128 devices in a mesh: pr: 4 (over x), pc: 32 (over y, z, core).
Axes of the slice: x: 4, y: 4, z: 4, core: 2. Of those that a mesh axis runs over, the one named last changes fastest.
Arguments:
- matrix: float32 [4, 8, 512, 32, 1, 512], P('pr', None, None, 'pc'), may hold values from -8 to 9, as said below
Outputs:
- factored: float32 [4, 8, 512, 32, 1, 512], P('pr', None, None, 'pc')
The draws below stay inside these ranges and needn't reach their ends.
Inputs may be any that keep to these rules, and one draw needn't show every extreme that they name: The matrix A that matrix stores is symmetric and positive definite.
All inputs are finite; a program needn't handle non-finite values.
Results may differ from the reference program's by a relative error of at most 0.00012.
Values sent between devices are 32-bit elements; how exact they have to be, the bound alone decides.
A program may use at most 128 MiB of HBM per device.

```python
import math
import jax
import jax.numpy as jnp
from jax import lax

NB = 512
LC = 1
STEPS = 2
PROWS = 4
PCOLS = 32
LR = 8
N = 16384


def draw_matrix(key, part):
    key_angle, key_radius, key_noise = jax.random.split(key, 3)
    angle = jax.random.uniform(key_angle, (N,), jnp.float32, 0.0, 2.0 * math.pi)
    radius = jax.random.uniform(key_radius, (N,), jnp.float32, 1.0, 2.0)
    xs = radius * jnp.cos(angle)
    ys = radius * jnp.sin(angle)
    spread = math.sqrt(60.0 / N)
    dist_sq = (xs[:, None] - xs[None, :]) ** 2 + (ys[:, None] - ys[None, :]) ** 2
    kernel = jnp.exp(-dist_sq / (2.0 * spread * spread))
    noise = jax.random.normal(key_noise, (N, N), jnp.float32)
    sym_noise = (noise + noise.T) * (0.25 / math.sqrt(2.0 * N))
    full = jnp.eye(N, dtype=jnp.float32) + kernel + sym_noise
    return full.reshape(LR, PROWS, NB, LC, PCOLS, NB).transpose(1, 0, 2, 4, 3, 5)


def setup_inputs(seed: int = 0) -> dict:
    key_of = jax.random.split(jax.random.key(seed), 2)
    return {
        "matrix": draw_matrix(jax.random.fold_in(key_of[1], 71), 0),
    }


def reference(matrix):
    full = matrix.transpose(1, 0, 2, 4, 3, 5).reshape(N, N)
    eye = jnp.eye(NB, dtype=jnp.float32)
    dims = (((1,), (1,)), ((), ()))
    for step in range(STEPS):
        low = step * NB
        high = low + NB
        factor = jnp.tril(jnp.linalg.cholesky(full[low:high, low:high]))
        inverse = jax.scipy.linalg.solve_triangular(factor, eye, lower=True)
        panel = lax.dot_general(full[high:, low:high].astype(jnp.float32), inverse.astype(jnp.float32), dims, precision=lax.Precision.HIGHEST, preferred_element_type=jnp.float32)
        update = lax.dot_general(panel.astype(jnp.float32), panel.astype(jnp.float32), dims, precision=lax.Precision.HIGHEST, preferred_element_type=jnp.float32)
        full = full.at[high:, high:].set(full[high:, high:] - update)
        full = full.at[high:, low:high].set(panel)
        full = full.at[low:high, low:high].set(factor)
        full = full.at[low:high, high:].set(panel.T)
    return full.reshape(LR, PROWS, NB, LC, PCOLS, NB).transpose(1, 0, 2, 4, 3, 5)
```

```python
import jax
import jax.numpy as jnp
from jax import lax
from jax.experimental import pallas as pl
from jax.experimental.pallas import tpu as pltpu
from jax.sharding import PartitionSpec as P
HI = lax.Precision.HIGHEST
T = 128
NT = 8
NB = 512
N2 = 1024


def dot(a, b, ca=1, cb=0):
    return lax.dot_general(a, b, (((ca,), (cb,)), ((), ())), precision=HI, preferred_element_type=jnp.float32)


def sub_bcast(x, j):
    return jnp.broadcast_to(x[j : j + 1, :], (8, T))


def lane_bcast(x, j):
    return jnp.broadcast_to(x[:, j : j + 1], (8, T))


def factor_tile(rows):
    sub = lax.broadcasted_iota(jnp.int32, (8, T), 0)
    lane = lax.broadcasted_iota(jnp.int32, (8, T), 1)
    inv_rows, fac_rows = [], []
    for b in range(T // 8):
        r0 = 8 * b
        low = rows[b]
        full = rows[b]
        cols = [lane_bcast(rows[b], r0 + j) for j in range(8)]
        later = {i: [lane_bcast(rows[i], r0 + j) for j in range(8)] for i in range(b + 1, T // 8)}
        dvec = jnp.zeros((8, T), jnp.float32)
        rvec = jnp.zeros((8, T), jnp.float32)
        for j in range(8):
            d = sub_bcast(cols[j], j)
            rinv = 1.0 / d
            f = cols[j] * rinv
            here = lane == r0 + j
            fg = jnp.where(sub == j, 0.0, f)
            fl = jnp.where(sub > j, f, 0.0)
            for jj in range(j + 1, 8):
                cols[jj] = cols[jj] - fg * sub_bcast(cols[jj], j)
            low_now = jnp.where(here & (sub > j), 0.0, low)
            lrow = jnp.where(here, 1.0, sub_bcast(low, j))
            low = low_now - fl * lrow
            grow = jnp.where(here, 1.0, sub_bcast(full, j))
            full = jnp.where(here, jnp.where(sub == j, 1.0, 0.0), full) - fg * grow
            dvec = jnp.where(sub == j, d, dvec)
            rvec = jnp.where(sub == j, rinv, rvec)
        full = full * rvec
        pieces = [sub_bcast(full, j) for j in range(8)]
        inblk = (lane >= r0) & (lane < r0 + 8)
        for i in range(b + 1, T // 8):
            acc = jnp.where(inblk, 0.0, rows[i])
            for j in range(8):
                acc = acc - later[i][j] * pieces[j]
            rows[i] = acc
        rs = lax.rsqrt(dvec)
        rs = rs * (1.5 - 0.5 * dvec * rs * rs)
        row = sub + r0
        scaled = low * rs
        inv_rows.append(jnp.where(lane < row, scaled, jnp.where(lane == row, rs, 0.0)))
        fac_rows.append(jnp.where(lane >= row, scaled, 0.0))
    return inv_rows, fac_rows


def factor_kernel(s_ref, b_ref, top_ref, q_ref, m, u_ref, g_ref, w_ref):
    pr = lax.axis_index("pr")
    pc = lax.axis_index("pc")
    m[0:NB, 0:NB] = s_ref[0]
    m[0:NB, NB:] = s_ref[1]
    m[NB:, NB:] = s_ref[2]

    @pl.loop(0, NT)
    def _(t):
        o = pl.multiple_of(t * T, T)
        rows = [m[pl.ds(o + 8 * i, 8), pl.ds(o, T)] for i in range(T // 8)]
        inv_rows, fac_rows = factor_tile(rows)
        for i in range(T // 8):
            g_ref[pl.ds(o + 8 * i, 8), :] = inv_rows[i]
            u_ref[pl.ds(o + 8 * i, 8), pl.ds(o, T)] = fac_rows[i]
        for ts in range(NT - 1):

            @pl.when(t == ts)
            def _():
                a, b = ts * T, (ts + 1) * T
                u = dot(g_ref[a:b, :], m[a:b, b:])
                u_ref[a:b, b:] = u
                for i in range(ts + 1, NT):
                    lo = (i - ts - 1) * T
                    m[i * T : (i + 1) * T, i * T :] -= dot(u[:, lo : lo + T], u[:, lo:], 0, 0)

    for t in range(NT):
        a, b = t * T, (t + 1) * T
        acc = b_ref[a:b, :]
        if t:
            acc = acc - dot(u_ref[0:a, a:b], w_ref[0:a, :], 0, 0)
        w_ref[a:b, :] = dot(g_ref[a:b, :], acc)

    top_ref[...] = w_ref[pl.ds(pl.multiple_of(jnp.minimum(pr, 1) * NB, NB), NB), :]
    for k in range(2):

        @pl.when((pc == k) & (pr == k))
        def _():
            for i in range(NB // T):
                for j in range(NB // T):
                    a, b = k * NB + i * T, k * NB + j * T
                    if j <= i:
                        piece = u_ref[b : b + T, a : a + T].T
                    else:
                        piece = jnp.zeros((T, T), jnp.float32)
                    top_ref[i * T : (i + 1) * T, j * T : (j + 1) * T] = piece

    @pl.when(pc < 2)
    def _():
        row = lax.broadcasted_iota(jnp.int32, (N2, NB), 0)
        col = lax.broadcasted_iota(jnp.int32, (N2, NB), 1)
        w_ref[...] = jnp.where(row == col + pc * NB, -1.0, 0.0)

    for t in reversed(range(NT)):
        a, b = t * T, (t + 1) * T
        acc = w_ref[a:b, :]
        if t < NT - 1:
            acc = acc - dot(u_ref[a:b, b:], q_ref[b:, :])
        q_ref[a:b, :] = dot(g_ref[a:b, :], acc, 0, 0)


def factor(s, b):
    vmem = pl.BlockSpec(memory_space=pltpu.VMEM)
    return pl.pallas_call(
        factor_kernel,
        out_shape=(jax.ShapeDtypeStruct((NB, NB), jnp.float32), jax.ShapeDtypeStruct((N2, NB), jnp.float32)),
        in_specs=[vmem, vmem],
        out_specs=(vmem, vmem),
        scratch_shapes=[
            pltpu.VMEM((N2, N2), jnp.float32),
            pltpu.VMEM((N2, N2), jnp.float32),
            pltpu.VMEM((N2, T), jnp.float32),
            pltpu.VMEM((N2, NB), jnp.float32),
        ],
        compiler_params=pltpu.CompilerParams(vmem_limit_bytes=48 << 20),
        cost_estimate=pl.CostEstimate(flops=40_000_000_000, bytes_accessed=10_000_000, transcendentals=0),
    )(s, b)


def split(x):
    hi = x.astype(jnp.bfloat16)
    return hi, (x - hi.astype(jnp.float32)).astype(jnp.bfloat16)


def mm(a, b):
    return lax.dot_general(a, b, (((1,), (0,)), ((), ())), preferred_element_type=jnp.float32)


def update_kernel(a_ref, p_ref, q_ref, top_ref, o_ref, qh, ql):
    l = pl.program_id(0)
    pr = lax.axis_index("pr")
    pc = lax.axis_index("pc")

    @pl.when(l == 0)
    def _():
        qh[...], ql[...] = split(q_ref[...])

    keep = jnp.where(pc < 2, 0.0, 1.0)
    acc = None
    for k in range(2):
        ph, plo = split(p_ref[:, k].reshape(NB, NB))
        h, lo = qh[k * NB : (k + 1) * NB], ql[k * NB : (k + 1) * NB]
        part = mm(ph, h) + (mm(ph, lo) + mm(plo, h))
        acc = part if acc is None else acc + part
    for c in range(4):
        at = pl.ds(c, NB, stride=4)
        o_ref[at, :] = keep * a_ref[at, :] - acc[:, c * T : (c + 1) * T]

    @pl.when((l == 0) & ((pr == 0) | ((pr == 1) & (pc > 0))))
    def _():
        for c in range(4):
            o_ref[pl.ds(c, NB, stride=4), :] = top_ref[:, c * T : (c + 1) * T]


def update(a, p, q, top):
    return pl.pallas_call(
        update_kernel,
        grid=(8,),
        out_shape=jax.ShapeDtypeStruct(a.shape, jnp.float32),
        in_specs=[
            pl.BlockSpec((4 * NB, T), lambda l: (l, 0)),
            pl.BlockSpec((4, 2, T, NB), lambda l: (l, 0, 0, 0)),
            pl.BlockSpec((N2, NB), lambda l: (0, 0)),
            pl.BlockSpec((NB, NB), lambda l: (0, 0)),
        ],
        out_specs=pl.BlockSpec((4 * NB, T), lambda l: (l, 0)),
        scratch_shapes=[pltpu.VMEM((N2, NB), jnp.bfloat16), pltpu.VMEM((N2, NB), jnp.bfloat16)],
        compiler_params=pltpu.CompilerParams(vmem_limit_bytes=48 << 20),
        cost_estimate=pl.CostEstimate(flops=13_000_000_000, bytes_accessed=34_000_000, transcendentals=0),
    )(a, p, q, top)


def body(matrix):
    flat = matrix.reshape(8 * NB * 4, T)
    first = matrix[0, 0].reshape(NB, NB)
    pr = lax.axis_index("pr")
    pc = lax.axis_index("pc")
    owner = [(pr == 0) & (pc == 0), (pr == 0) & (pc == 1), (pr == 1) & (pc == 1)]
    s = lax.psum(jnp.stack([jnp.where(o, first, 0.0) for o in owner]), ("pr", "pc"))
    b = lax.all_gather(first, "pr")[:2].reshape(N2, NB)
    turned = first.T
    mine = []
    for k in range(2):
        got = None
        for part in range(4):
            pairs = [(k * 32 + i, (i % 4) * 32 + 4 * (i // 4) + part) for i in range(32)]
            one = lax.ppermute(turned[part * T : (part + 1) * T], ("pr", "pc"), pairs)
            got = one if got is None else got + one
        mine.append(got)
    panel = lax.all_gather(jnp.stack(mine), "pc")
    top, q = factor(s, b)
    return update(flat, panel, q, top).reshape(matrix.shape)


def solution(mesh):
    return jax.shard_map(
        body,
        mesh=mesh,
        in_specs=(P("pr", None, None, "pc", None, None),),
        out_specs=P("pr", None, None, "pc", None, None),
        check_vma=False,
    )
```

```python
import jax
import jax.numpy as jnp
from jax import lax
from jax.experimental import pallas as pl
from jax.experimental.pallas import tpu as pltpu
from jax.sharding import PartitionSpec as P
HI = lax.Precision.HIGHEST
T = 128
NT = 8
NB = 512
N2 = 1024
MESH = pl.DeviceIdType.MESH
ROOTS = ((0, 0), (0, 1), (1, 1))


def dot(a, b, ca=1, cb=0):
    return lax.dot_general(a, b, (((ca,), (cb,)), ((), ())), precision=HI, preferred_element_type=jnp.float32)


def sub_bcast(x, j):
    return jnp.broadcast_to(x[j : j + 1, :], (8, T))


def lane_bcast(x, j):
    return jnp.broadcast_to(x[:, j : j + 1], (8, T))


def factor_tile(rows):
    sub = lax.broadcasted_iota(jnp.int32, (8, T), 0)
    lane = lax.broadcasted_iota(jnp.int32, (8, T), 1)
    inv_rows, fac_rows = [], []
    for b in range(T // 8):
        r0 = 8 * b
        low = rows[b]
        full = rows[b]
        cols = [lane_bcast(rows[b], r0 + j) for j in range(8)]
        later = {i: [lane_bcast(rows[i], r0 + j) for j in range(8)] for i in range(b + 1, T // 8)}
        dvec = jnp.zeros((8, T), jnp.float32)
        rvec = jnp.zeros((8, T), jnp.float32)
        for j in range(8):
            d = sub_bcast(cols[j], j)
            rinv = 1.0 / d
            f = cols[j] * rinv
            here = lane == r0 + j
            fg = jnp.where(sub == j, 0.0, f)
            fl = jnp.where(sub > j, f, 0.0)
            for jj in range(j + 1, 8):
                cols[jj] = cols[jj] - fg * sub_bcast(cols[jj], j)
            low_now = jnp.where(here & (sub > j), 0.0, low)
            lrow = jnp.where(here, 1.0, sub_bcast(low, j))
            low = low_now - fl * lrow
            grow = jnp.where(here, 1.0, sub_bcast(full, j))
            full = jnp.where(here, jnp.where(sub == j, 1.0, 0.0), full) - fg * grow
            dvec = jnp.where(sub == j, d, dvec)
            rvec = jnp.where(sub == j, rinv, rvec)
        full = full * rvec
        pieces = [sub_bcast(full, j) for j in range(8)]
        inblk = (lane >= r0) & (lane < r0 + 8)
        for i in range(b + 1, T // 8):
            acc = jnp.where(inblk, 0.0, rows[i])
            for j in range(8):
                acc = acc - later[i][j] * pieces[j]
            rows[i] = acc
        rs = lax.rsqrt(dvec)
        rs = rs * (1.5 - 0.5 * dvec * rs * rs)
        row = sub + r0
        scaled = low * rs
        inv_rows.append(jnp.where(lane < row, scaled, jnp.where(lane == row, rs, 0.0)))
        fac_rows.append(jnp.where(lane >= row, scaled, 0.0))
    return inv_rows, fac_rows


class Links:
    def __init__(self, a, sbuf, bbuf, local, scat_s, scat_r, x_s, x_r, ag_s, ag_r, b_s, b_r):
        self.a, self.sbuf, self.bbuf, self.local = a, sbuf, bbuf, local
        self.scat_s, self.scat_r, self.x_s, self.x_r = scat_s, scat_r, x_s, x_r
        self.ag_s, self.ag_r, self.b_s, self.b_r = ag_s, ag_r, b_s, b_r
        self.pr, self.pc = lax.axis_index("pr"), lax.axis_index("pc")
        self.y, self.z, self.c = self.pc // 8, (self.pc // 2) % 4, self.pc % 2

    def copy(self, src, dst, send, recv, pr, pc):
        return pltpu.make_async_remote_copy(
            src_ref=src, dst_ref=dst, send_sem=send, recv_sem=recv, device_id={"pr": pr, "pc": pc}, device_id_type=MESH
        )

    def place(self, y, z, c):
        return (y * 4 + z) * 2 + c

    def barrier(self):
        sem = pltpu.get_barrier_semaphore()

        def signal(pr, pc):
            pl.semaphore_signal(sem, inc=1, device_id={"pr": pr, "pc": pc}, device_id_type=MESH)

        for n in range(1, 4):
            signal((self.pr + n) % 4, self.pc)
            signal(self.pr, self.place((self.y + n) % 4, self.z, self.c))
            signal(self.pr, self.place(self.y, (self.z + n) % 4, self.c))
        signal(self.pr, self.place(self.y, self.z, 1 - self.c))
        roots = [(self.pr == p) & (self.pc == q) for p, q in ROOTS]
        for p, q in ROOTS:

            @pl.when((self.pr == p) & (self.pc != q))
            def _():
                signal(p, q)

        is_root = roots[0] | roots[1] | roots[2]

        @pl.when(is_root)
        def _():
            pl.semaphore_wait(sem, 41)

        @pl.when(jnp.logical_not(is_root))
        def _():
            pl.semaphore_wait(sem, 10)

    def slab(self, x, d):
        return self.sbuf.at[x, d // 8, (d // 2) % 4, d % 2]

    def scatter_copy(self, x, d):
        src = self.a.at[pl.ds(pl.multiple_of(d * 64, 64), 64)]
        return self.copy(src, self.slab(x, d), self.scat_s.at[d], self.scat_r.at[x], ROOTS[x][0], d)

    def own_copy(self, x):
        d = ROOTS[x][1]
        return pltpu.make_async_copy(self.a.at[pl.ds(d * 64, 64)], self.slab(x, d), self.local.at[0])

    def each_other(self, x, act):
        p, q = ROOTS[x]

        @pl.when((self.pr == p) & (self.pc == q))
        def _():
            @pl.loop(0, 32)
            def _(d):
                @pl.when(d != q)
                def _():
                    act(self.scatter_copy(x, d))

    def scatter_start(self, x):
        p, q = ROOTS[x]
        self.each_other(x, lambda copy: copy.start())

        @pl.when((self.pr == p) & (self.pc == q))
        def _():
            self.own_copy(x).start()

    def x_copy(self, x, n):
        mine = self.slab(x, self.pc)
        return self.copy(mine, mine, self.x_s.at[x, n - 1], self.x_r.at[x], (self.pr + n) % 4, self.pc)

    def spread_start(self, x):
        p, q = ROOTS[x]

        @pl.when((self.pr == p) & (self.pc == q))
        def _():
            self.own_copy(x).wait()

        @pl.when((self.pr == p) & (self.pc != q))
        def _():
            self.scatter_copy(x, self.pc).wait_recv()

        @pl.when(self.pr == p)
        def _():
            for n in range(1, 4):
                self.x_copy(x, n).start()

    def spread_wait(self, x):
        @pl.when(self.pr != ROOTS[x][0])
        def _():
            self.x_copy(x, 1).wait_recv()

    def gather_copies(self, x, phase, arriving=False):
        y, z, c = self.y, self.z, self.c
        if phase == 2:
            oc = 1 - c
            ref = self.sbuf.at[x, :, :, oc if arriving else c]
            return [self.copy(ref, ref, self.ag_s.at[x, 12], self.ag_r.at[x, 12], self.pr, self.place(y, z, oc))]
        out = []
        for n in range(1, 4):
            m = (4 - n) % 4 if arriving else 0
            ym, zm = (y + m) % 4, (z + m) % 4
            if phase == 0:
                first = self.sbuf.at[x, ym, z, c, pl.ds(0, 32)]
                second = self.sbuf.at[x, y, zm, c, pl.ds(32, 32)]
                to_first, to_second = self.place((y + n) % 4, z, c), self.place(y, (z + n) % 4, c)
            else:
                first = self.sbuf.at[x, :, zm, c, pl.ds(0, 32)]
                second = self.sbuf.at[x, ym, :, c, pl.ds(32, 32)]
                to_first, to_second = self.place(y, (z + n) % 4, c), self.place((y + n) % 4, z, c)
            k = phase * 6 + (n - 1) * 2
            out.append(self.copy(first, first, self.ag_s.at[x, k], self.ag_r.at[x, k], self.pr, to_first))
            out.append(self.copy(second, second, self.ag_s.at[x, k + 1], self.ag_r.at[x, k + 1], self.pr, to_second))
        return out

    def gather_start(self, x, phase):
        for copy in self.gather_copies(x, phase):
            copy.start()

    def gather_wait(self, x, phase):
        for copy in self.gather_copies(x, phase, arriving=True):
            copy.wait_recv()

    def b_copy(self, k, n):
        return self.copy(
            self.a.at[pl.ds(0, 4 * NB)], self.bbuf.at[k], self.b_s.at[n - 1], self.b_r.at[k], (self.pr + n) % 4, self.pc
        )

    def b_own(self, k):
        return pltpu.make_async_copy(self.a.at[pl.ds(0, 4 * NB)], self.bbuf.at[k], self.local.at[1])

    def b_start(self):
        for k in range(2):

            @pl.when(self.pr == k)
            def _():
                self.b_own(k).start()
                for n in range(1, 4):
                    self.b_copy(k, n).start()

    def b_wait(self):
        for k in range(2):

            @pl.when(self.pr == k)
            def _():
                self.b_own(k).wait()

            @pl.when(self.pr != k)
            def _():
                self.b_copy(k, 1).wait_recv()

    def finish(self):
        for x in range(3):
            self.each_other(x, lambda copy: copy.wait_send())

            @pl.when(self.pr == ROOTS[x][0])
            def _():
                for n in range(1, 4):
                    self.x_copy(x, n).wait_send()

            for phase in range(3):
                for copy in self.gather_copies(x, phase):
                    copy.wait_send()
        for k in range(2):

            @pl.when(self.pr == k)
            def _():
                for n in range(1, 4):
                    self.b_copy(k, n).wait_send()


def spread_rows(ref):
    return [ref[pl.ds(c, NB, stride=4), :] for c in range(4)]


def factor_kernel(a_ref, top_ref, q_ref, sbuf, bbuf, m, u, g, r, x, w, *sems):
    net = Links(a_ref, sbuf, bbuf, *sems)
    pr, pc = net.pr, net.pc
    flat = sbuf.reshape(3, 4 * NB, T)
    net.barrier()
    net.scatter_start(0)
    net.spread_start(0)
    net.scatter_start(1)
    net.scatter_start(2)
    net.spread_wait(0)
    net.gather_start(0, 0)
    net.gather_wait(0, 0)
    net.gather_start(0, 1)
    net.spread_start(1)
    net.spread_start(2)
    net.gather_wait(0, 1)
    net.gather_start(0, 2)
    net.gather_wait(0, 2)
    for c, piece in enumerate(spread_rows(flat.at[0])):
        m[0:NB, c * T : (c + 1) * T] = piece

    def after(t):
        if t == 0:
            for i in (1, 2):
                net.spread_wait(i)
                net.gather_start(i, 0)
            net.b_start()
        elif t < 3:
            for i in (1, 2):
                net.gather_wait(i, t - 1)
                net.gather_start(i, t)

    def solve_second():
        for i in (1, 2):
            net.gather_wait(i, 2)
        net.b_wait()
        for c, piece in enumerate(spread_rows(flat.at[1])):
            r[:, c * T : (c + 1) * T] = piece
        for c, piece in enumerate(spread_rows(bbuf.at[0])):
            r[:, NB + c * T : NB + (c + 1) * T] = piece
        for t in range(4):
            a, b = t * T, (t + 1) * T
            acc = r[a:b, :]
            if t:
                acc = acc - dot(u[0:a, a:b], x[0:a, :], 0, 0)
            x[a:b, :] = dot(g[a:b, :], acc)
        r[...] = dot(x[:, 0:NB], x[...], 0, 0)
        for c, piece in enumerate(spread_rows(flat.at[2])):
            m[NB:, c * T : (c + 1) * T] = piece - r[:, c * T : (c + 1) * T]
        for c, piece in enumerate(spread_rows(bbuf.at[1])):
            w[NB:, c * T : (c + 1) * T] = piece - r[:, NB + c * T : NB + (c + 1) * T]

    @pl.loop(0, NT)
    def _(t):
        o = pl.multiple_of(t * T, T)
        oc = pl.multiple_of((t % 4) * T, T)
        rows = [m[pl.ds(o + 8 * i, 8), pl.ds(oc, T)] for i in range(T // 8)]
        inv_rows, fac_rows = factor_tile(rows)
        for i in range(T // 8):
            g[pl.ds(o + 8 * i, 8), :] = inv_rows[i]
            u[pl.ds(o + 8 * i, 8), pl.ds(oc, T)] = fac_rows[i]
        for ts in range(NT - 1):

            @pl.when(t == ts)
            def _():
                if ts == 3:
                    solve_second()
                    return
                base = ts // 4 * NB
                a, b = ts % 4 * T, (ts % 4 + 1) * T
                piece = dot(g[base + a : base + b, :], m[base + a : base + b, b:])
                u[base + a : base + b, b:] = piece
                for i in range(ts % 4 + 1, 4):
                    lo = i * T - b
                    m[base + i * T : base + (i + 1) * T, i * T :] -= dot(piece[:, lo : lo + T], piece[:, lo:], 0, 0)
                after(ts)

    w[0:NB, :] = x[:, NB:]
    for t in range(4):
        a, b = t * T, (t + 1) * T
        acc = w[NB + a : NB + b, :]
        if t:
            acc = acc - dot(u[NB : NB + a, a:b], w[NB : NB + a, :], 0, 0)
        w[NB + a : NB + b, :] = dot(g[NB + a : NB + b, :], acc)

    top_ref[...] = w[pl.ds(pl.multiple_of(jnp.minimum(pr, 1) * NB, NB), NB), :]
    for k in range(2):

        @pl.when((pc == k) & (pr == k))
        def _():
            for i in range(NB // T):
                for j in range(NB // T):
                    if j <= i:
                        piece = u[k * NB + j * T : k * NB + (j + 1) * T, i * T : (i + 1) * T].T
                    else:
                        piece = jnp.zeros((T, T), jnp.float32)
                    top_ref[i * T : (i + 1) * T, j * T : (j + 1) * T] = piece

    @pl.when(pc < 2)
    def _():
        row = lax.broadcasted_iota(jnp.int32, (N2, NB), 0)
        col = lax.broadcasted_iota(jnp.int32, (N2, NB), 1)
        w[...] = jnp.where(row == col + pc * NB, -1.0, 0.0)

    for half in (NB, 0):
        if half == 0:
            w[0:NB, :] = w[0:NB, :] - dot(x[:, 0:NB], q_ref[NB:, :])
        for t in reversed(range(4)):
            a, b = t * T, (t + 1) * T
            acc = w[half + a : half + b, :]
            if t < 3:
                acc = acc - dot(u[half + a : half + b, b:], q_ref[half + b : half + NB, :])
            q_ref[half + a : half + b, :] = dot(g[half + a : half + b, :], acc, 0, 0)
    net.finish()


def factor(a):
    vmem = pl.BlockSpec(memory_space=pltpu.VMEM)
    f32 = jnp.float32
    dma = pltpu.SemaphoreType.DMA
    return pl.pallas_call(
        factor_kernel,
        out_shape=(jax.ShapeDtypeStruct((NB, NB), f32), jax.ShapeDtypeStruct((N2, NB), f32)),
        in_specs=[pl.BlockSpec(memory_space=pl.ANY)],
        out_specs=(vmem, vmem),
        scratch_shapes=[
            pltpu.VMEM((3, 4, 4, 2, 64, T), f32),
            pltpu.VMEM((2, 4 * NB, T), f32),
            pltpu.VMEM((N2, NB), f32),
            pltpu.VMEM((N2, NB), f32),
            pltpu.VMEM((N2, T), f32),
            pltpu.VMEM((NB, N2), f32),
            pltpu.VMEM((NB, N2), f32),
            pltpu.VMEM((N2, NB), f32),
            dma((2,)),
            dma((32,)),
            dma((3,)),
            dma((3, 3)),
            dma((3,)),
            dma((3, 13)),
            dma((3, 13)),
            dma((3,)),
            dma((2,)),
        ],
        compiler_params=pltpu.CompilerParams(vmem_limit_bytes=48 << 20, collective_id=0, has_side_effects=True),
        cost_estimate=pl.CostEstimate(flops=60_000_000_000, bytes_accessed=10_000_000, transcendentals=0),
    )(a)


def split(x):
    hi = x.astype(jnp.bfloat16)
    return hi, (x - hi.astype(jnp.float32)).astype(jnp.bfloat16)


def mm(a, b):
    return lax.dot_general(a, b, (((1,), (0,)), ((), ())), preferred_element_type=jnp.float32)


def update_kernel(a_ref, p_ref, q_ref, top_ref, o_ref, qh, ql):
    l = pl.program_id(0)
    pr = lax.axis_index("pr")
    pc = lax.axis_index("pc")

    @pl.when(l == 0)
    def _():
        qh[...], ql[...] = split(q_ref[...])

    keep = jnp.where(pc < 2, 0.0, 1.0)
    acc = None
    for k in range(2):
        ph, plo = split(p_ref[:, k].reshape(NB, NB))
        h, lo = qh[k * NB : (k + 1) * NB], ql[k * NB : (k + 1) * NB]
        part = mm(ph, h) + (mm(ph, lo) + mm(plo, h))
        acc = part if acc is None else acc + part
    for c in range(4):
        at = pl.ds(c, NB, stride=4)
        o_ref[at, :] = keep * a_ref[at, :] - acc[:, c * T : (c + 1) * T]

    @pl.when((l == 0) & ((pr == 0) | ((pr == 1) & (pc > 0))))
    def _():
        for c in range(4):
            o_ref[pl.ds(c, NB, stride=4), :] = top_ref[:, c * T : (c + 1) * T]


def update(a, p, q, top):
    return pl.pallas_call(
        update_kernel,
        grid=(8,),
        out_shape=jax.ShapeDtypeStruct(a.shape, jnp.float32),
        in_specs=[
            pl.BlockSpec((4 * NB, T), lambda l: (l, 0)),
            pl.BlockSpec((4, 2, T, NB), lambda l: (l, 0, 0, 0)),
            pl.BlockSpec((N2, NB), lambda l: (0, 0)),
            pl.BlockSpec((NB, NB), lambda l: (0, 0)),
        ],
        out_specs=pl.BlockSpec((4 * NB, T), lambda l: (l, 0)),
        scratch_shapes=[pltpu.VMEM((N2, NB), jnp.bfloat16), pltpu.VMEM((N2, NB), jnp.bfloat16)],
        compiler_params=pltpu.CompilerParams(vmem_limit_bytes=48 << 20),
        cost_estimate=pl.CostEstimate(flops=13_000_000_000, bytes_accessed=34_000_000, transcendentals=0),
    )(a, p, q, top)


def body(matrix):
    flat = matrix.reshape(8 * NB * 4, T)
    first = matrix[0, 0].reshape(NB, NB)
    turned = first.T
    mine = []
    for k in range(2):
        got = None
        for part in range(4):
            pairs = [(k * 32 + i, (i % 4) * 32 + 4 * (i // 4) + part) for i in range(32)]
            one = lax.ppermute(turned[part * T : (part + 1) * T], ("pr", "pc"), pairs)
            got = one if got is None else got + one
        mine.append(got)
    panel = lax.all_gather(jnp.stack(mine), "pc")
    top, q = factor(flat)
    return update(flat, panel, q, top).reshape(matrix.shape)


def solution(mesh):
    return jax.shard_map(
        body,
        mesh=mesh,
        in_specs=(P("pr", None, None, "pc", None, None),),
        out_specs=P("pr", None, None, "pc", None, None),
        check_vma=False,
    )
```

```python
import jax
import jax.numpy as jnp
from jax import lax
from jax.experimental import pallas as pl
from jax.experimental.pallas import tpu as pltpu
from jax.sharding import PartitionSpec as P
HI = lax.Precision.HIGHEST
T = 128
NT = 8
NB = 512
N2 = 1024
MESH = pl.DeviceIdType.MESH
ROOTS = ((0, 0), (0, 1), (1, 1))


def dot(a, b, ca=1, cb=0):
    return lax.dot_general(a, b, (((ca,), (cb,)), ((), ())), precision=HI, preferred_element_type=jnp.float32)


def sub_bcast(x, j):
    return jnp.broadcast_to(x[j : j + 1, :], (8, T))


def lane_bcast(x, j):
    return jnp.broadcast_to(x[:, j : j + 1], (8, T))


def factor_tile(rows):
    sub = lax.broadcasted_iota(jnp.int32, (8, T), 0)
    lane = lax.broadcasted_iota(jnp.int32, (8, T), 1)
    inv_rows, fac_rows = [], []
    for b in range(T // 8):
        r0 = 8 * b
        low = rows[b]
        full = rows[b]
        cols = [lane_bcast(rows[b], r0 + j) for j in range(8)]
        later = {i: [lane_bcast(rows[i], r0 + j) for j in range(8)] for i in range(b + 1, T // 8)}
        dvec = jnp.zeros((8, T), jnp.float32)
        rvec = jnp.zeros((8, T), jnp.float32)
        for j in range(8):
            d = sub_bcast(cols[j], j)
            rinv = 1.0 / d
            f = cols[j] * rinv
            here = lane == r0 + j
            fg = jnp.where(sub == j, 0.0, f)
            fl = jnp.where(sub > j, f, 0.0)
            for jj in range(j + 1, 8):
                cols[jj] = cols[jj] - fg * sub_bcast(cols[jj], j)
            low_now = jnp.where(here & (sub > j), 0.0, low)
            lrow = jnp.where(here, 1.0, sub_bcast(low, j))
            low = low_now - fl * lrow
            grow = jnp.where(here, 1.0, sub_bcast(full, j))
            full = jnp.where(here, jnp.where(sub == j, 1.0, 0.0), full) - fg * grow
            dvec = jnp.where(sub == j, d, dvec)
            rvec = jnp.where(sub == j, rinv, rvec)
        full = full * rvec
        pieces = [sub_bcast(full, j) for j in range(8)]
        inblk = (lane >= r0) & (lane < r0 + 8)
        for i in range(b + 1, T // 8):
            acc = jnp.where(inblk, 0.0, rows[i])
            for j in range(8):
                acc = acc - later[i][j] * pieces[j]
            rows[i] = acc
        rs = lax.rsqrt(dvec)
        rs = rs * (1.5 - 0.5 * dvec * rs * rs)
        row = sub + r0
        scaled = low * rs
        inv_rows.append(jnp.where(lane < row, scaled, jnp.where(lane == row, rs, 0.0)))
        fac_rows.append(jnp.where(lane >= row, scaled, 0.0))
    return inv_rows, fac_rows


class Links:
    def __init__(self, a, pan, sbuf, bbuf, tbuf, local, scat_s, scat_r, x_s, x_r, ag_s, ag_r, b_s, b_r, t_s, t_r, p_s, p_r, c_s, c_r):
        self.a, self.sbuf, self.bbuf, self.local = a, sbuf, bbuf, local
        self.pan, self.tbuf, self.t_s, self.t_r = pan, tbuf, t_s, t_r
        self.p_s, self.p_r, self.c_s, self.c_r = p_s, p_r, c_s, c_r
        self.scat_s, self.scat_r, self.x_s, self.x_r = scat_s, scat_r, x_s, x_r
        self.ag_s, self.ag_r, self.b_s, self.b_r = ag_s, ag_r, b_s, b_r
        self.pr, self.pc = lax.axis_index("pr"), lax.axis_index("pc")
        self.y, self.z, self.c = self.pc // 8, (self.pc // 2) % 4, self.pc % 2
        self.row_owner = self.pr < 2
        self.dst_pr = self.pc % 4
        self.dst_z = 2 * (self.z // 2) + (self.pr + self.z) % 2
        self.keeps = (self.pr == 0) & (self.dst_pr == 0)
        self.src_pr = (self.z + self.pr // 2) % 2
        self.src_pc = self.place(self.y, 2 * (self.z // 2) + self.pr // 2, self.pr % 2)
        self.from_self = (self.src_pr == self.pr) & (self.src_pc == self.pc)

    def copy(self, src, dst, send, recv, pr, pc):
        return pltpu.make_async_remote_copy(
            src_ref=src, dst_ref=dst, send_sem=send, recv_sem=recv, device_id={"pr": pr, "pc": pc}, device_id_type=MESH
        )

    def place(self, y, z, c):
        return (y * 4 + z) * 2 + c

    def barrier(self):
        sem = pltpu.get_barrier_semaphore()

        def signal(pr, pc):
            pl.semaphore_signal(sem, inc=1, device_id={"pr": pr, "pc": pc}, device_id_type=MESH)

        for n in range(1, 4):
            signal((self.pr + n) % 4, self.pc)
            signal(self.pr, self.place((self.y + n) % 4, self.z, self.c))
            signal(self.pr, self.place(self.y, (self.z + n) % 4, self.c))
        signal(self.pr, self.place(self.y, self.z, 1 - self.c))
        roots = [(self.pr == p) & (self.pc == q) for p, q in ROOTS]
        for p, q in ROOTS:

            @pl.when((self.pr == p) & (self.pc != q))
            def _():
                signal(p, q)

        @pl.when(jnp.logical_not(self.from_self))
        def _():
            signal(self.src_pr, self.src_pc)

        is_root = roots[0] | roots[1] | roots[2]

        sources = self.row_owner & jnp.logical_not(self.keeps)
        other = jnp.logical_not(is_root)
        for base, group in ((41, is_root), (10, other)):
            for more, kind in ((2, sources), (1, self.keeps), (0, jnp.logical_not(self.row_owner))):

                @pl.when(group & kind)
                def _():
                    pl.semaphore_wait(sem, base + more)

    def slab(self, x, d):
        return self.sbuf.at[x, d // 8, (d // 2) % 4, d % 2]

    def scatter_copy(self, x, d):
        src = self.a.at[pl.ds(pl.multiple_of(d * 64, 64), 64)]
        return self.copy(src, self.slab(x, d), self.scat_s.at[d], self.scat_r.at[x], ROOTS[x][0], d)

    def own_copy(self, x):
        d = ROOTS[x][1]
        return pltpu.make_async_copy(self.a.at[pl.ds(d * 64, 64)], self.slab(x, d), self.local.at[0])

    def each_other(self, x, act):
        p, q = ROOTS[x]

        @pl.when((self.pr == p) & (self.pc == q))
        def _():
            @pl.loop(0, 32)
            def _(d):
                @pl.when(d != q)
                def _():
                    act(self.scatter_copy(x, d))

    def scatter_start(self, x):
        p, q = ROOTS[x]
        self.each_other(x, lambda copy: copy.start())

        @pl.when((self.pr == p) & (self.pc == q))
        def _():
            self.own_copy(x).start()

    def x_copy(self, x, n):
        mine = self.slab(x, self.pc)
        return self.copy(mine, mine, self.x_s.at[x, n - 1], self.x_r.at[x], (self.pr + n) % 4, self.pc)

    def spread_start(self, x):
        p, q = ROOTS[x]

        @pl.when((self.pr == p) & (self.pc == q))
        def _():
            self.own_copy(x).wait()

        @pl.when((self.pr == p) & (self.pc != q))
        def _():
            self.scatter_copy(x, self.pc).wait_recv()

        @pl.when(self.pr == p)
        def _():
            for n in range(1, 4):
                self.x_copy(x, n).start()

    def spread_wait(self, x):
        @pl.when(self.pr != ROOTS[x][0])
        def _():
            self.x_copy(x, 1).wait_recv()

    def gather_copies(self, x, phase, arriving=False):
        y, z, c = self.y, self.z, self.c
        if phase == 2:
            oc = 1 - c
            ref = self.sbuf.at[x, :, :, oc if arriving else c]
            return [self.copy(ref, ref, self.ag_s.at[x, 12], self.ag_r.at[x, 12], self.pr, self.place(y, z, oc))]
        out = []
        for n in range(1, 4):
            m = (4 - n) % 4 if arriving else 0
            ym, zm = (y + m) % 4, (z + m) % 4
            if phase == 0:
                first = self.sbuf.at[x, ym, z, c, pl.ds(0, 32)]
                second = self.sbuf.at[x, y, zm, c, pl.ds(32, 32)]
                to_first, to_second = self.place((y + n) % 4, z, c), self.place(y, (z + n) % 4, c)
            else:
                first = self.sbuf.at[x, :, zm, c, pl.ds(0, 32)]
                second = self.sbuf.at[x, ym, :, c, pl.ds(32, 32)]
                to_first, to_second = self.place(y, (z + n) % 4, c), self.place((y + n) % 4, z, c)
            k = phase * 6 + (n - 1) * 2
            out.append(self.copy(first, first, self.ag_s.at[x, k], self.ag_r.at[x, k], self.pr, to_first))
            out.append(self.copy(second, second, self.ag_s.at[x, k + 1], self.ag_r.at[x, k + 1], self.pr, to_second))
        return out

    def gather_start(self, x, phase):
        for copy in self.gather_copies(x, phase):
            copy.start()

    def gather_wait(self, x, phase):
        for copy in self.gather_copies(x, phase, arriving=True):
            copy.wait_recv()

    def b_copy(self, k, n):
        return self.copy(
            self.a.at[pl.ds(0, 4 * NB)], self.bbuf.at[k], self.b_s.at[n - 1], self.b_r.at[k], (self.pr + n) % 4, self.pc
        )

    def b_own(self, k):
        return pltpu.make_async_copy(self.a.at[pl.ds(0, 4 * NB)], self.bbuf.at[k], self.local.at[1])

    def own_start(self):
        for k in range(2):

            @pl.when(self.pr == k)
            def _():
                self.b_own(k).start()

    def turn(self):
        for k in range(2):

            @pl.when(self.pr == k)
            def _():
                self.b_own(k).wait()
                for s in range(4):
                    self.tbuf[s] = self.bbuf.at[k][pl.ds(s, NB, stride=4), :].T

    def t_refs(self, s, core):
        return self.tbuf.at[s, pl.ds(core * 64, 64)], self.pan.at[self.y, self.dst_z, s, core]

    def t_copy(self, s, core):
        src, dst = self.t_refs(s, core)
        to = self.place(self.y, self.dst_z, core)
        return self.copy(src, dst, self.t_s.at[s, core], self.t_r.at[s], self.dst_pr, to)

    def t_local(self, s):
        src, dst = self.t_refs(s, 0)
        return pltpu.make_async_copy(src, dst, self.local.at[2 + s])

    def t_start(self, s):
        @pl.when(self.keeps)
        def _():
            self.t_local(s).start()

        @pl.when(self.row_owner & jnp.logical_not(self.keeps))
        def _():
            self.t_copy(s, 0).start()

        @pl.when(self.row_owner)
        def _():
            self.t_copy(s, 1).start()

    def t_wait(self, s):
        @pl.when(self.from_self)
        def _():
            self.t_local(s).wait()

        @pl.when(jnp.logical_not(self.from_self))
        def _():
            mine = self.pan.at[self.y, self.z, s, self.c]
            self.copy(mine, mine, self.t_s.at[s, 0], self.t_r.at[s], self.src_pr, self.src_pc).wait_recv()

    def ring_part(self, s, order, phase, v, half):
        first, rows = (0, 32) if half is None else (16 * half, 16)
        at = pl.ds(32 * order + first, rows)
        along_y = (order + phase) % 2 == 0
        if phase == 0:
            return self.pan.at[v, self.z, s, self.c, at] if along_y else self.pan.at[self.y, v, s, self.c, at]
        return self.pan.at[v, :, s, self.c, at] if along_y else self.pan.at[:, v, s, self.c, at]

    def ring_copies(self, s, phase, step, arriving=False):
        out = []
        for order in range(2):
            along_y = (order + phase) % 2 == 0
            me = self.y if along_y else self.z
            for way in range(2):
                n = 1 if way == 0 else 3
                to = (me + n) % 4
                dev = self.place(to, self.z, self.c) if along_y else self.place(self.y, to, self.c)
                back = (step + 1 if arriving else step) * (4 - n)
                ref = self.ring_part(s, order, phase, (me + back) % 4, None if step == 0 else way)
                k = ((order * 2 + phase) * 2 + step) * 2 + way
                out.append(self.copy(ref, ref, self.p_s.at[s, k], self.p_r.at[s, k], self.pr, dev))
        return out

    def core_copy(self, s, arriving=False):
        oc = 1 - self.c
        ref = self.pan.at[:, :, s, oc if arriving else self.c]
        return self.copy(ref, ref, self.c_s.at[s], self.c_r.at[s], self.pr, self.place(self.y, self.z, oc))

    def panel_stage(self, s, stage):
        if stage == 0:
            self.t_start(s)
            return
        if stage == 1:
            self.t_wait(s)
        elif stage < 6:
            for copy in self.ring_copies(s, (stage - 2) // 2, (stage - 2) % 2, arriving=True):
                copy.wait_recv()
        else:
            self.core_copy(s, arriving=True).wait_recv()
            return
        if stage < 5:
            for copy in self.ring_copies(s, (stage - 1) // 2, (stage - 1) % 2):
                copy.start()
        else:
            self.core_copy(s).start()

    def panel_slot(self, slot):
        for s in range(4):
            if 0 <= slot - s <= 6:
                self.panel_stage(s, slot - s)

    def b_start(self):
        for k in range(2):

            @pl.when(self.pr == k)
            def _():
                for n in range(1, 4):
                    self.b_copy(k, n).start()

    def b_wait(self):
        for k in range(2):

            @pl.when(self.pr != k)
            def _():
                self.b_copy(k, 1).wait_recv()

    def finish(self):
        for s in range(4):

            @pl.when(self.row_owner & jnp.logical_not(self.keeps))
            def _():
                self.t_copy(s, 0).wait_send()

            @pl.when(self.row_owner)
            def _():
                self.t_copy(s, 1).wait_send()

            for phase in range(2):
                for step in range(2):
                    for copy in self.ring_copies(s, phase, step):
                        copy.wait_send()
            self.core_copy(s).wait_send()
        for x in range(3):
            self.each_other(x, lambda copy: copy.wait_send())

            @pl.when(self.pr == ROOTS[x][0])
            def _():
                for n in range(1, 4):
                    self.x_copy(x, n).wait_send()

            for phase in range(3):
                for copy in self.gather_copies(x, phase):
                    copy.wait_send()
        for k in range(2):

            @pl.when(self.pr == k)
            def _():
                for n in range(1, 4):
                    self.b_copy(k, n).wait_send()


def spread_rows(ref):
    return [ref[pl.ds(c, NB, stride=4), :] for c in range(4)]


def factor_kernel(a_ref, top_ref, q_ref, pan, sbuf, bbuf, tbuf, m, u, g, r, x, w, *sems):
    net = Links(a_ref, pan, sbuf, bbuf, tbuf, *sems)
    pr, pc = net.pr, net.pc
    flat = sbuf.reshape(3, 4 * NB, T)
    net.own_start()
    net.barrier()
    net.scatter_start(0)
    net.turn()
    net.spread_start(0)
    net.scatter_start(1)
    net.scatter_start(2)
    net.spread_wait(0)
    net.gather_start(0, 0)
    net.gather_wait(0, 0)
    net.gather_start(0, 1)
    net.spread_start(1)
    net.spread_start(2)
    net.gather_wait(0, 1)
    net.gather_start(0, 2)
    net.panel_slot(0)
    net.gather_wait(0, 2)
    for c, piece in enumerate(spread_rows(flat.at[0])):
        m[0:NB, c * T : (c + 1) * T] = piece

    def after(t):
        if t == 0:
            for i in (1, 2):
                net.spread_wait(i)
                net.gather_start(i, 0)
        elif t < 3:
            for i in (1, 2):
                net.gather_wait(i, t - 1)
                net.gather_start(i, t)
        net.panel_slot(t + 1)
        if t == 2:
            net.b_start()

    def forward(lo, dst, rhs):
        for t in range(4):
            a, b = t * T, (t + 1) * T
            acc = rhs[a:b, :]
            if t:
                acc = acc - dot(u[lo : lo + a, a:b], dst[0:a, :], 0, 0)
            dst[a:b, :] = dot(g[lo + a : lo + b, :], acc)

    def solve_second():
        for i in (1, 2):
            net.gather_wait(i, 2)
        for c, piece in enumerate(spread_rows(flat.at[1])):
            r[:, c * T : (c + 1) * T] = piece
        forward(0, x, r)
        r[...] = dot(x[...], x[...], 0, 0)
        for c, piece in enumerate(spread_rows(flat.at[2])):
            m[NB:, c * T : (c + 1) * T] = piece - r[:, c * T : (c + 1) * T]

    @pl.loop(0, NT)
    def _(t):
        o = pl.multiple_of(t * T, T)
        oc = pl.multiple_of((t % 4) * T, T)
        rows = [m[pl.ds(o + 8 * i, 8), pl.ds(oc, T)] for i in range(T // 8)]
        inv_rows, fac_rows = factor_tile(rows)
        for i in range(T // 8):
            g[pl.ds(o + 8 * i, 8), :] = inv_rows[i]
            u[pl.ds(o + 8 * i, 8), pl.ds(oc, T)] = fac_rows[i]
        for ts in range(NT):

            @pl.when(t == ts)
            def _():
                if ts % 4 == 3:
                    if ts == 3:
                        solve_second()
                    after(ts)
                    return
                base = ts // 4 * NB
                a, b = ts % 4 * T, (ts % 4 + 1) * T
                piece = dot(g[base + a : base + b, :], m[base + a : base + b, b:])
                u[base + a : base + b, b:] = piece
                for i in range(ts % 4 + 1, 4):
                    lo = i * T - b
                    m[base + i * T : base + (i + 1) * T, i * T :] -= dot(piece[:, lo : lo + T], piece[:, lo:], 0, 0)
                after(ts)

    net.b_wait()
    for c, piece in enumerate(spread_rows(bbuf.at[0])):
        r[:, c * T : (c + 1) * T] = piece
    forward(0, w.at[0:NB], r)
    r[...] = dot(x[...], w[0:NB, :], 0, 0)
    for c, piece in enumerate(spread_rows(bbuf.at[1])):
        r[:, c * T : (c + 1) * T] = piece - r[:, c * T : (c + 1) * T]
    forward(NB, w.at[NB:N2], r)

    top_ref[...] = w[pl.ds(pl.multiple_of(jnp.minimum(pr, 1) * NB, NB), NB), :]
    for k in range(2):

        @pl.when((pc == k) & (pr == k))
        def _():
            for i in range(NB // T):
                for j in range(NB // T):
                    if j <= i:
                        piece = u[k * NB + j * T : k * NB + (j + 1) * T, i * T : (i + 1) * T].T
                    else:
                        piece = jnp.zeros((T, T), jnp.float32)
                    top_ref[i * T : (i + 1) * T, j * T : (j + 1) * T] = piece

    @pl.when(pc < 2)
    def _():
        row = lax.broadcasted_iota(jnp.int32, (N2, NB), 0)
        col = lax.broadcasted_iota(jnp.int32, (N2, NB), 1)
        w[...] = jnp.where(row == col + pc * NB, -1.0, 0.0)

    for half in (NB, 0):
        if half == 0:
            w[0:NB, :] = w[0:NB, :] - dot(x[...], q_ref[NB:, :])
        for t in reversed(range(4)):
            a, b = t * T, (t + 1) * T
            acc = w[half + a : half + b, :]
            if t < 3:
                acc = acc - dot(u[half + a : half + b, b:], q_ref[half + b : half + NB, :])
            q_ref[half + a : half + b, :] = dot(g[half + a : half + b, :], acc, 0, 0)
    net.panel_slot(9)
    net.finish()


def factor(a):
    vmem = pl.BlockSpec(memory_space=pltpu.VMEM)
    f32 = jnp.float32
    dma = pltpu.SemaphoreType.DMA
    return pl.pallas_call(
        factor_kernel,
        out_shape=(
            jax.ShapeDtypeStruct((NB, NB), f32),
            jax.ShapeDtypeStruct((N2, NB), f32),
            jax.ShapeDtypeStruct((4, 4, 4, 2, 64, NB), f32),
        ),
        in_specs=[pl.BlockSpec(memory_space=pl.ANY)],
        out_specs=(vmem, vmem, pl.BlockSpec(memory_space=pl.ANY)),
        scratch_shapes=[
            pltpu.VMEM((3, 4, 4, 2, 64, T), f32),
            pltpu.VMEM((2, 4 * NB, T), f32),
            pltpu.VMEM((4, T, NB), f32),
            pltpu.VMEM((N2, NB), f32),
            pltpu.VMEM((N2, NB), f32),
            pltpu.VMEM((N2, T), f32),
            pltpu.VMEM((NB, NB), f32),
            pltpu.VMEM((NB, NB), f32),
            pltpu.VMEM((N2, NB), f32),
            dma((6,)),
            dma((32,)),
            dma((3,)),
            dma((3, 3)),
            dma((3,)),
            dma((3, 13)),
            dma((3, 13)),
            dma((3,)),
            dma((2,)),
            dma((4, 2)),
            dma((4,)),
            dma((4, 16)),
            dma((4, 16)),
            dma((4,)),
            dma((4,)),
        ],
        compiler_params=pltpu.CompilerParams(vmem_limit_bytes=48 << 20, collective_id=0, has_side_effects=True),
        cost_estimate=pl.CostEstimate(flops=60_000_000_000, bytes_accessed=10_000_000, transcendentals=0),
    )(a)


def split(x):
    hi = x.astype(jnp.bfloat16)
    return hi, (x - hi.astype(jnp.float32)).astype(jnp.bfloat16)


def mm(a, b):
    return lax.dot_general(a, b, (((1,), (0,)), ((), ())), preferred_element_type=jnp.float32)


def update_kernel(a_ref, p_ref, q_ref, top_ref, o_ref, qh, ql):
    l = pl.program_id(0)
    pr = lax.axis_index("pr")
    pc = lax.axis_index("pc")

    @pl.when(l == 0)
    def _():
        qh[...], ql[...] = split(q_ref[...])

    keep = jnp.where(pc < 2, 0.0, 1.0)
    acc = None
    for k in range(2):
        ph, plo = split(p_ref[0, k])
        at = pl.ds(pl.multiple_of((k + pr // 2) % 2 * NB, NB), NB)
        h, lo = qh[at, :], ql[at, :]
        part = mm(ph, h) + (mm(ph, lo) + mm(plo, h))
        acc = part if acc is None else acc + part
    for c in range(4):
        at = pl.ds(c, NB, stride=4)
        o_ref[at, :] = keep * a_ref[at, :] - acc[:, c * T : (c + 1) * T]

    @pl.when((l == 0) & ((pr == 0) | ((pr == 1) & (pc > 0))))
    def _():
        for c in range(4):
            o_ref[pl.ds(c, NB, stride=4), :] = top_ref[:, c * T : (c + 1) * T]


def update(a, p, q, top):
    return pl.pallas_call(
        update_kernel,
        grid=(8,),
        out_shape=jax.ShapeDtypeStruct(a.shape, jnp.float32),
        in_specs=[
            pl.BlockSpec((4 * NB, T), lambda l: (l, 0)),
            pl.BlockSpec((1, 2, NB, NB), lambda l: (l, 0, 0, 0)),
            pl.BlockSpec((N2, NB), lambda l: (0, 0)),
            pl.BlockSpec((NB, NB), lambda l: (0, 0)),
        ],
        out_specs=pl.BlockSpec((4 * NB, T), lambda l: (l, 0)),
        scratch_shapes=[pltpu.VMEM((N2, NB), jnp.bfloat16), pltpu.VMEM((N2, NB), jnp.bfloat16)],
        compiler_params=pltpu.CompilerParams(vmem_limit_bytes=48 << 20),
        cost_estimate=pl.CostEstimate(flops=13_000_000_000, bytes_accessed=34_000_000, transcendentals=0),
    )(a, p, q, top)


def body(matrix):
    flat = matrix.reshape(8 * NB * 4, T)
    top, q, panel = factor(flat)
    panel = panel.reshape(8, 2, NB, NB)
    return update(flat, panel, q, top).reshape(matrix.shape)


def solution(mesh):
    return jax.shard_map(
        body,
        mesh=mesh,
        in_specs=(P("pr", None, None, "pc", None, None),),
        out_specs=P("pr", None, None, "pc", None, None),
        check_vma=False,
    )
```

```python
import jax
import jax.numpy as jnp
from jax import lax
from jax.experimental import pallas as pl
from jax.experimental.pallas import tpu as pltpu
from jax.sharding import PartitionSpec as P
HI = lax.Precision.HIGHEST
T = 128
NT = 8
NB = 512
N2 = 1024
MESH = pl.DeviceIdType.MESH
ROOTS = ((0, 0), (0, 1), (1, 1))


def dot(a, b, ca=1, cb=0):
    return lax.dot_general(a, b, (((ca,), (cb,)), ((), ())), precision=HI, preferred_element_type=jnp.float32)


def sub_bcast(x, j):
    return jnp.broadcast_to(x[j : j + 1, :], (8, T))


def lane_bcast(x, j):
    return jnp.broadcast_to(x[:, j : j + 1], (8, T))


def factor_tile(rows):
    sub = lax.broadcasted_iota(jnp.int32, (8, T), 0)
    lane = lax.broadcasted_iota(jnp.int32, (8, T), 1)
    inv_rows, fac_rows = [], []
    for b in range(T // 8):
        r0 = 8 * b
        low = rows[b]
        full = rows[b]
        cols = [lane_bcast(rows[b], r0 + j) for j in range(8)]
        later = {i: [lane_bcast(rows[i], r0 + j) for j in range(8)] for i in range(b + 1, T // 8)}
        dvec = jnp.zeros((8, T), jnp.float32)
        rvec = jnp.zeros((8, T), jnp.float32)
        for j in range(8):
            d = sub_bcast(cols[j], j)
            rinv = 1.0 / d
            f = cols[j] * rinv
            here = lane == r0 + j
            fg = jnp.where(sub == j, 0.0, f)
            fl = jnp.where(sub > j, f, 0.0)
            for jj in range(j + 1, 8):
                cols[jj] = cols[jj] - fg * sub_bcast(cols[jj], j)
            low_now = jnp.where(here & (sub > j), 0.0, low)
            lrow = jnp.where(here, 1.0, sub_bcast(low, j))
            low = low_now - fl * lrow
            grow = jnp.where(here, 1.0, sub_bcast(full, j))
            full = jnp.where(here, jnp.where(sub == j, 1.0, 0.0), full) - fg * grow
            dvec = jnp.where(sub == j, d, dvec)
            rvec = jnp.where(sub == j, rinv, rvec)
        full = full * rvec
        pieces = [sub_bcast(full, j) for j in range(8)]
        inblk = (lane >= r0) & (lane < r0 + 8)
        for i in range(b + 1, T // 8):
            acc = jnp.where(inblk, 0.0, rows[i])
            for j in range(8):
                acc = acc - later[i][j] * pieces[j]
            rows[i] = acc
        rs = lax.rsqrt(dvec)
        rs = rs * (1.5 - 0.5 * dvec * rs * rs)
        row = sub + r0
        scaled = low * rs
        inv_rows.append(jnp.where(lane < row, scaled, jnp.where(lane == row, rs, 0.0)))
        fac_rows.append(jnp.where(lane >= row, scaled, 0.0))
    return inv_rows, fac_rows


class Links:
    def __init__(self, a, pan, sbuf, abuf, bt, local, scat_s, scat_r, x_s, x_r, ag_s, ag_r, b_s, b_r, f_s, t_s, t_r, p_s, p_r, c_s, c_r):
        self.a, self.sbuf, self.abuf, self.bt, self.local = a, sbuf, abuf, bt, local
        self.pan, self.f_s, self.t_s, self.t_r = pan, f_s, t_s, t_r
        self.p_s, self.p_r, self.c_s, self.c_r = p_s, p_r, c_s, c_r
        self.scat_s, self.scat_r, self.x_s, self.x_r = scat_s, scat_r, x_s, x_r
        self.ag_s, self.ag_r, self.b_s, self.b_r = ag_s, ag_r, b_s, b_r
        self.pr, self.pc = lax.axis_index("pr"), lax.axis_index("pc")
        self.y, self.z, self.c = self.pc // 8, (self.pc // 2) % 4, self.pc % 2
        self.owner = self.pr == self.pc % 4
        self.src_pc = self.place(self.y, 2 * (self.z // 2) + self.pr // 2, self.pr % 2)
        self.from_self = self.src_pc == self.pc

    def copy(self, src, dst, send, recv, pr, pc):
        return pltpu.make_async_remote_copy(
            src_ref=src, dst_ref=dst, send_sem=send, recv_sem=recv, device_id={"pr": pr, "pc": pc}, device_id_type=MESH
        )

    def place(self, y, z, c):
        return (y * 4 + z) * 2 + c

    def barrier(self):
        sem = pltpu.get_barrier_semaphore()

        def signal(pr, pc):
            pl.semaphore_signal(sem, inc=1, device_id={"pr": pr, "pc": pc}, device_id_type=MESH)

        for n in range(1, 4):
            signal((self.pr + n) % 4, self.pc)
            signal(self.pr, self.place((self.y + n) % 4, self.z, self.c))
            signal(self.pr, self.place(self.y, (self.z + n) % 4, self.c))
        signal(self.pr, self.place(self.y, self.z, 1 - self.c))
        roots = [(self.pr == p) & (self.pc == q) for p, q in ROOTS]
        for p, q in ROOTS:

            @pl.when((self.pr == p) & (self.pc != q))
            def _():
                signal(p, q)

        @pl.when(jnp.logical_not(self.from_self))
        def _():
            signal(self.pr, self.src_pc)

        is_root = roots[0] | roots[1] | roots[2]

        for base, group in ((41, is_root), (10, jnp.logical_not(is_root))):
            for more, kind in ((3, self.owner), (0, jnp.logical_not(self.owner))):

                @pl.when(group & kind)
                def _():
                    pl.semaphore_wait(sem, base + more)

    def slab(self, x, d):
        return self.sbuf.at[x, d // 8, (d // 2) % 4, d % 2]

    def scatter_copy(self, x, d):
        src = self.a.at[pl.ds(pl.multiple_of(d * 64, 64), 64)]
        return self.copy(src, self.slab(x, d), self.scat_s.at[d], self.scat_r.at[x], ROOTS[x][0], d)

    def own_copy(self, x):
        d = ROOTS[x][1]
        return pltpu.make_async_copy(self.a.at[pl.ds(d * 64, 64)], self.slab(x, d), self.local.at[0])

    def each_other(self, x, act):
        p, q = ROOTS[x]

        @pl.when((self.pr == p) & (self.pc == q))
        def _():
            @pl.loop(0, 32)
            def _(d):
                @pl.when(d != q)
                def _():
                    act(self.scatter_copy(x, d))

    def scatter_start(self, x):
        p, q = ROOTS[x]
        self.each_other(x, lambda copy: copy.start())

        @pl.when((self.pr == p) & (self.pc == q))
        def _():
            self.own_copy(x).start()

    def x_copy(self, x, n):
        mine = self.slab(x, self.pc)
        return self.copy(mine, mine, self.x_s.at[x, n - 1], self.x_r.at[x], (self.pr + n) % 4, self.pc)

    def spread_start(self, x):
        p, q = ROOTS[x]

        @pl.when((self.pr == p) & (self.pc == q))
        def _():
            self.own_copy(x).wait()

        @pl.when((self.pr == p) & (self.pc != q))
        def _():
            self.scatter_copy(x, self.pc).wait_recv()

        @pl.when(self.pr == p)
        def _():
            for n in range(1, 4):
                self.x_copy(x, n).start()

    def spread_wait(self, x):
        @pl.when(self.pr != ROOTS[x][0])
        def _():
            self.x_copy(x, 1).wait_recv()

    def gather_copies(self, x, phase, arriving=False):
        y, z, c = self.y, self.z, self.c
        if phase == 2:
            oc = 1 - c
            ref = self.sbuf.at[x, :, :, oc if arriving else c]
            return [self.copy(ref, ref, self.ag_s.at[x, 12], self.ag_r.at[x, 12], self.pr, self.place(y, z, oc))]
        out = []
        for n in range(1, 4):
            m = (4 - n) % 4 if arriving else 0
            ym, zm = (y + m) % 4, (z + m) % 4
            if phase == 0:
                first = self.sbuf.at[x, ym, z, c, pl.ds(0, 32)]
                second = self.sbuf.at[x, y, zm, c, pl.ds(32, 32)]
                to_first, to_second = self.place((y + n) % 4, z, c), self.place(y, (z + n) % 4, c)
            else:
                first = self.sbuf.at[x, :, zm, c, pl.ds(0, 32)]
                second = self.sbuf.at[x, ym, :, c, pl.ds(32, 32)]
                to_first, to_second = self.place(y, (z + n) % 4, c), self.place((y + n) % 4, z, c)
            k = phase * 6 + (n - 1) * 2
            out.append(self.copy(first, first, self.ag_s.at[x, k], self.ag_r.at[x, k], self.pr, to_first))
            out.append(self.copy(second, second, self.ag_s.at[x, k + 1], self.ag_r.at[x, k + 1], self.pr, to_second))
        return out

    def gather_start(self, x, phase):
        for copy in self.gather_copies(x, phase):
            copy.start()

    def gather_wait(self, x, phase):
        for copy in self.gather_copies(x, phase, arriving=True):
            copy.wait_recv()

    def own_copy_in(self):
        return pltpu.make_async_copy(self.a.at[pl.ds(0, 4 * NB)], self.abuf, self.local.at[1])

    def own_start(self):
        @pl.when(self.pr < 2)
        def _():
            self.own_copy_in().start()

    def turn(self):
        for k in range(2):

            @pl.when(self.pr == k)
            def _():
                self.own_copy_in().wait()
                for s in range(4):
                    self.bt[k, s] = self.abuf[pl.ds(s, NB, stride=4), :].T

    def b_copy(self, k, s, way):
        ref, n = self.bt.at[k, s], 3 if way else 1
        return self.copy(ref, ref, self.b_s.at[s, way], self.b_r.at[k, s, 0], (self.pr + n) % 4, self.pc)

    def f_copy(self, k, s, way):
        ref, n = self.bt.at[k, s, pl.ds(64 * way, 64)], 3 if way else 1
        return self.copy(ref, ref, self.f_s.at[k, s], self.b_r.at[k, s, way], (self.pr + n) % 4, self.pc)

    def at_distance(self, k, n):
        return self.pr == (k + n) % 4

    def b_start(self, s):
        for k in range(2):

            @pl.when(self.at_distance(k, 0))
            def _():
                for way in range(2):
                    self.b_copy(k, s, way).start()

    def b_forward(self, s):
        for k in range(2):
            for way, n in ((0, 1), (1, 3)):

                @pl.when(self.at_distance(k, n))
                def _():
                    self.b_copy(k, s, way).wait_recv()
                    self.f_copy(k, s, way).start()

    def b_wait(self, s):
        for k in range(2):

            @pl.when(self.at_distance(k, 2))
            def _():
                for way in range(2):
                    self.f_copy(k, s, way).wait_recv()

    def b_finish(self, s):
        for k in range(2):

            @pl.when(self.at_distance(k, 0))
            def _():
                for way in range(2):
                    self.b_copy(k, s, way).wait_send()

            for way, n in ((0, 1), (1, 3)):

                @pl.when(self.at_distance(k, n))
                def _():
                    self.f_copy(k, s, way).wait_send()

    def t_half(self, k, s, core):
        z = self.z if k == 0 else 2 * (self.z // 2) + 1 - self.z % 2
        return self.bt.at[k, s, pl.ds(core * 64, 64)], self.pan.at[self.y, z, s, core], z

    def t_local(self, s):
        src, dst, _ = self.t_half(0, s, self.c)
        return pltpu.make_async_copy(src, dst, self.local.at[2 + s])

    def t_copies(self, s):
        out = []
        for i, (k, core) in enumerate(((0, 1 - self.c), (1, 0), (1, 1))):
            src, dst, z = self.t_half(k, s, core)
            out.append(self.copy(src, dst, self.t_s.at[s, i], self.t_r.at[s], self.pr, self.place(self.y, z, core)))
        return out

    def t_start(self, s):
        @pl.when(self.owner)
        def _():
            self.t_local(s).start()
            for copy in self.t_copies(s):
                copy.start()

    def t_wait(self, s):
        @pl.when(self.from_self)
        def _():
            self.t_local(s).wait()

        @pl.when(jnp.logical_not(self.from_self))
        def _():
            mine = self.pan.at[self.y, self.z, s, self.c]
            self.copy(mine, mine, self.t_s.at[s, 0], self.t_r.at[s], self.pr, self.src_pc).wait_recv()

    def ring_part(self, s, order, phase, v, half):
        first, rows = (0, 32) if half is None else (16 * half, 16)
        at = pl.ds(32 * order + first, rows)
        along_y = (order + phase) % 2 == 0
        if phase == 0:
            return self.pan.at[v, self.z, s, self.c, at] if along_y else self.pan.at[self.y, v, s, self.c, at]
        return self.pan.at[v, :, s, self.c, at] if along_y else self.pan.at[:, v, s, self.c, at]

    def ring_copies(self, s, phase, step, arriving=False):
        out = []
        for order in range(2):
            along_y = (order + phase) % 2 == 0
            me = self.y if along_y else self.z
            for way in range(2):
                n = 1 if way == 0 else 3
                to = (me + n) % 4
                dev = self.place(to, self.z, self.c) if along_y else self.place(self.y, to, self.c)
                back = (step + 1 if arriving else step) * (4 - n)
                ref = self.ring_part(s, order, phase, (me + back) % 4, None if step == 0 else way)
                k = ((order * 2 + phase) * 2 + step) * 2 + way
                out.append(self.copy(ref, ref, self.p_s.at[s, k], self.p_r.at[s, k], self.pr, dev))
        return out

    def core_copy(self, s, arriving=False):
        oc = 1 - self.c
        ref = self.pan.at[:, :, s, oc if arriving else self.c]
        return self.copy(ref, ref, self.c_s.at[s], self.c_r.at[s], self.pr, self.place(self.y, self.z, oc))

    def panel_stage(self, s, stage):
        if stage == 0:
            self.b_start(s)
        elif stage == 1:
            self.b_forward(s)
        elif stage == 2:
            self.b_wait(s)
            self.t_start(s)
        elif stage == 3:
            self.t_wait(s)
        elif stage < 8:
            for copy in self.ring_copies(s, (stage - 4) // 2, stage % 2, arriving=True):
                copy.wait_recv()
        else:
            self.core_copy(s, arriving=True).wait_recv()
        if 3 <= stage < 7:
            for copy in self.ring_copies(s, (stage - 3) // 2, (stage - 3) % 2):
                copy.start()
        elif stage == 7:
            self.core_copy(s).start()

    def panel_slot(self, slot):
        for s in range(4):
            if 0 <= slot - s <= 8:
                self.panel_stage(s, slot - s)

    def finish(self):
        for s in range(4):

            self.b_finish(s)

            @pl.when(self.owner)
            def _():
                for copy in self.t_copies(s):
                    copy.wait_send()

            for phase in range(2):
                for step in range(2):
                    for copy in self.ring_copies(s, phase, step):
                        copy.wait_send()
            self.core_copy(s).wait_send()
        for x in range(3):
            self.each_other(x, lambda copy: copy.wait_send())

            @pl.when(self.pr == ROOTS[x][0])
            def _():
                for n in range(1, 4):
                    self.x_copy(x, n).wait_send()

            for phase in range(3):
                for copy in self.gather_copies(x, phase):
                    copy.wait_send()


def spread_rows(ref):
    return [ref[pl.ds(c, NB, stride=4), :] for c in range(4)]


def factor_kernel(a_ref, top_ref, q_ref, pan, sbuf, abuf, bt, m, u, g, r, x, w, *sems):
    net = Links(a_ref, pan, sbuf, abuf, bt, *sems)
    pr, pc = net.pr, net.pc
    flat = sbuf.reshape(3, 4 * NB, T)
    net.own_start()
    net.barrier()
    net.scatter_start(0)
    net.turn()
    net.panel_slot(0)
    net.spread_start(0)
    net.scatter_start(1)
    net.scatter_start(2)
    net.spread_wait(0)
    net.gather_start(0, 0)
    net.gather_wait(0, 0)
    net.gather_start(0, 1)
    net.spread_start(1)
    net.spread_start(2)
    net.gather_wait(0, 1)
    net.gather_start(0, 2)
    net.panel_slot(1)
    net.gather_wait(0, 2)
    for c, piece in enumerate(spread_rows(flat.at[0])):
        m[0:NB, c * T : (c + 1) * T] = piece

    def after(t):
        if t == 0:
            for i in (1, 2):
                net.spread_wait(i)
                net.gather_start(i, 0)
        elif t < 3:
            for i in (1, 2):
                net.gather_wait(i, t - 1)
                net.gather_start(i, t)
        net.panel_slot(t + 2)

    def forward(lo, dst, rhs):
        for t in range(4):
            a, b = t * T, (t + 1) * T
            acc = rhs[a:b, :]
            if t:
                acc = acc - dot(u[lo : lo + a, a:b], dst[0:a, :], 0, 0)
            dst[a:b, :] = dot(g[lo + a : lo + b, :], acc)

    def solve_second():
        for i in (1, 2):
            net.gather_wait(i, 2)
        for c, piece in enumerate(spread_rows(flat.at[1])):
            r[:, c * T : (c + 1) * T] = piece
        forward(0, x, r)
        r[...] = dot(x[...], x[...], 0, 0)
        for c, piece in enumerate(spread_rows(flat.at[2])):
            m[NB:, c * T : (c + 1) * T] = piece - r[:, c * T : (c + 1) * T]

    @pl.loop(0, NT)
    def _(t):
        o = pl.multiple_of(t * T, T)
        oc = pl.multiple_of((t % 4) * T, T)
        rows = [m[pl.ds(o + 8 * i, 8), pl.ds(oc, T)] for i in range(T // 8)]
        inv_rows, fac_rows = factor_tile(rows)
        for i in range(T // 8):
            g[pl.ds(o + 8 * i, 8), :] = inv_rows[i]
            u[pl.ds(o + 8 * i, 8), pl.ds(oc, T)] = fac_rows[i]
        for ts in range(NT):

            @pl.when(t == ts)
            def _():
                if ts % 4 == 3:
                    if ts == 3:
                        solve_second()
                    after(ts)
                    return
                base = ts // 4 * NB
                a, b = ts % 4 * T, (ts % 4 + 1) * T
                piece = dot(g[base + a : base + b, :], m[base + a : base + b, b:])
                u[base + a : base + b, b:] = piece
                for i in range(ts % 4 + 1, 4):
                    lo = i * T - b
                    m[base + i * T : base + (i + 1) * T, i * T :] -= dot(piece[:, lo : lo + T], piece[:, lo:], 0, 0)
                after(ts)

    for c in range(4):
        r[:, c * T : (c + 1) * T] = bt[0, c].T
    forward(0, w.at[0:NB], r)
    r[...] = dot(x[...], w[0:NB, :], 0, 0)
    for c in range(4):
        r[:, c * T : (c + 1) * T] = bt[1, c].T - r[:, c * T : (c + 1) * T]
    net.panel_slot(10)
    forward(NB, w.at[NB:N2], r)

    top_ref[...] = w[pl.ds(pl.multiple_of(jnp.minimum(pr, 1) * NB, NB), NB), :]
    for k in range(2):

        @pl.when((pc == k) & (pr == k))
        def _():
            for i in range(NB // T):
                for j in range(NB // T):
                    if j <= i:
                        piece = u[k * NB + j * T : k * NB + (j + 1) * T, i * T : (i + 1) * T].T
                    else:
                        piece = jnp.zeros((T, T), jnp.float32)
                    top_ref[i * T : (i + 1) * T, j * T : (j + 1) * T] = piece

    @pl.when(pc < 2)
    def _():
        row = lax.broadcasted_iota(jnp.int32, (N2, NB), 0)
        col = lax.broadcasted_iota(jnp.int32, (N2, NB), 1)
        w[...] = jnp.where(row == col + pc * NB, -1.0, 0.0)

    for half in (NB, 0):
        if half == 0:
            w[0:NB, :] = w[0:NB, :] - dot(x[...], q_ref[NB:, :])
        for t in reversed(range(4)):
            a, b = t * T, (t + 1) * T
            acc = w[half + a : half + b, :]
            if t < 3:
                acc = acc - dot(u[half + a : half + b, b:], q_ref[half + b : half + NB, :])
            q_ref[half + a : half + b, :] = dot(g[half + a : half + b, :], acc, 0, 0)
    net.panel_slot(11)
    net.finish()


def factor(a):
    vmem = pl.BlockSpec(memory_space=pltpu.VMEM)
    f32 = jnp.float32
    dma = pltpu.SemaphoreType.DMA
    return pl.pallas_call(
        factor_kernel,
        out_shape=(
            jax.ShapeDtypeStruct((NB, NB), f32),
            jax.ShapeDtypeStruct((N2, NB), f32),
            jax.ShapeDtypeStruct((4, 4, 4, 2, 64, NB), f32),
        ),
        in_specs=[pl.BlockSpec(memory_space=pl.ANY)],
        out_specs=(vmem, vmem, pl.BlockSpec(memory_space=pl.ANY)),
        scratch_shapes=[
            pltpu.VMEM((3, 4, 4, 2, 64, T), f32),
            pltpu.VMEM((4 * NB, T), f32),
            pltpu.VMEM((2, 4, T, NB), f32),
            pltpu.VMEM((N2, NB), f32),
            pltpu.VMEM((N2, NB), f32),
            pltpu.VMEM((N2, T), f32),
            pltpu.VMEM((NB, NB), f32),
            pltpu.VMEM((NB, NB), f32),
            pltpu.VMEM((N2, NB), f32),
            dma((6,)),
            dma((32,)),
            dma((3,)),
            dma((3, 3)),
            dma((3,)),
            dma((3, 13)),
            dma((3, 13)),
            dma((4, 2)),
            dma((2, 4, 2)),
            dma((2, 4)),
            dma((4, 3)),
            dma((4,)),
            dma((4, 16)),
            dma((4, 16)),
            dma((4,)),
            dma((4,)),
        ],
        compiler_params=pltpu.CompilerParams(vmem_limit_bytes=48 << 20, collective_id=0, has_side_effects=True),
        cost_estimate=pl.CostEstimate(flops=60_000_000_000, bytes_accessed=10_000_000, transcendentals=0),
    )(a)


def split(x):
    hi = x.astype(jnp.bfloat16)
    return hi, (x - hi.astype(jnp.float32)).astype(jnp.bfloat16)


def mm(a, b):
    return lax.dot_general(a, b, (((1,), (0,)), ((), ())), preferred_element_type=jnp.float32)


def update_kernel(a_ref, p_ref, q_ref, top_ref, o_ref, qh, ql):
    l = pl.program_id(0)
    pr = lax.axis_index("pr")
    pc = lax.axis_index("pc")

    @pl.when(l == 0)
    def _():
        qh[...], ql[...] = split(q_ref[...])

    keep = jnp.where(pc < 2, 0.0, 1.0)
    acc = None
    for k in range(2):
        ph, plo = split(p_ref[0, k])
        at = pl.ds(pl.multiple_of((k + pr // 2) % 2 * NB, NB), NB)
        h, lo = qh[at, :], ql[at, :]
        part = mm(ph, h) + (mm(ph, lo) + mm(plo, h))
        acc = part if acc is None else acc + part
    for c in range(4):
        at = pl.ds(c, NB, stride=4)
        o_ref[at, :] = keep * a_ref[at, :] - acc[:, c * T : (c + 1) * T]

    @pl.when((l == 0) & ((pr == 0) | ((pr == 1) & (pc > 0))))
    def _():
        for c in range(4):
            o_ref[pl.ds(c, NB, stride=4), :] = top_ref[:, c * T : (c + 1) * T]


def update(a, p, q, top):
    return pl.pallas_call(
        update_kernel,
        grid=(8,),
        out_shape=jax.ShapeDtypeStruct(a.shape, jnp.float32),
        in_specs=[
            pl.BlockSpec((4 * NB, T), lambda l: (l, 0)),
            pl.BlockSpec((1, 2, NB, NB), lambda l: (l, 0, 0, 0)),
            pl.BlockSpec((N2, NB), lambda l: (0, 0)),
            pl.BlockSpec((NB, NB), lambda l: (0, 0)),
        ],
        out_specs=pl.BlockSpec((4 * NB, T), lambda l: (l, 0)),
        scratch_shapes=[pltpu.VMEM((N2, NB), jnp.bfloat16), pltpu.VMEM((N2, NB), jnp.bfloat16)],
        compiler_params=pltpu.CompilerParams(vmem_limit_bytes=48 << 20),
        cost_estimate=pl.CostEstimate(flops=13_000_000_000, bytes_accessed=34_000_000, transcendentals=0),
    )(a, p, q, top)


def body(matrix):
    flat = matrix.reshape(8 * NB * 4, T)
    top, q, panel = factor(flat)
    panel = panel.reshape(8, 2, NB, NB)
    return update(flat, panel, q, top).reshape(matrix.shape)


def solution(mesh):
    return jax.shard_map(
        body,
        mesh=mesh,
        in_specs=(P("pr", None, None, "pc", None, None),),
        out_specs=P("pr", None, None, "pc", None, None),
        check_vma=False,
    )
```

```python
import jax
import jax.numpy as jnp
from jax import lax
from jax.experimental import pallas as pl
from jax.experimental.pallas import tpu as pltpu
from jax.sharding import PartitionSpec as P
HI = lax.Precision.HIGHEST
T = 128
NT = 8
NB = 512
N2 = 1024
MESH = pl.DeviceIdType.MESH
ROOTS = ((0, 0), (0, 1), (1, 1))


def dot(a, b, ca=1, cb=0):
    return lax.dot_general(a, b, (((ca,), (cb,)), ((), ())), precision=HI, preferred_element_type=jnp.float32)


def dot3(a, b, ca=1, cb=0):
    (ah, al), (bh, bl) = split(a), split(b)

    def one(p, q):
        return lax.dot_general(p, q, (((ca,), (cb,)), ((), ())), preferred_element_type=jnp.float32)

    return one(ah, bh) + (one(ah, bl) + one(al, bh))


def sub_bcast(x, j):
    return jnp.broadcast_to(x[j : j + 1, :], (8, T))


def lane_bcast(x, j):
    return jnp.broadcast_to(x[:, j : j + 1], (8, T))


def factor_tile(rows):
    sub = lax.broadcasted_iota(jnp.int32, (8, T), 0)
    lane = lax.broadcasted_iota(jnp.int32, (8, T), 1)
    inv_rows, fac_rows = [], []
    for b in range(T // 8):
        r0 = 8 * b
        low = rows[b]
        full = rows[b]
        cols = [lane_bcast(rows[b], r0 + j) for j in range(8)]
        later = {i: [lane_bcast(rows[i], r0 + j) for j in range(8)] for i in range(b + 1, T // 8)}
        dvec = jnp.zeros((8, T), jnp.float32)
        rvec = jnp.zeros((8, T), jnp.float32)
        for j in range(8):
            d = sub_bcast(cols[j], j)
            rinv = 1.0 / d
            f = cols[j] * rinv
            here = lane == r0 + j
            fg = jnp.where(sub == j, 0.0, f)
            fl = jnp.where(sub > j, f, 0.0)
            for jj in range(j + 1, 8):
                cols[jj] = cols[jj] - fg * sub_bcast(cols[jj], j)
            low_now = jnp.where(here & (sub > j), 0.0, low)
            lrow = jnp.where(here, 1.0, sub_bcast(low, j))
            low = low_now - fl * lrow
            grow = jnp.where(here, 1.0, sub_bcast(full, j))
            full = jnp.where(here, jnp.where(sub == j, 1.0, 0.0), full) - fg * grow
            dvec = jnp.where(sub == j, d, dvec)
            rvec = jnp.where(sub == j, rinv, rvec)
        full = full * rvec
        pieces = [sub_bcast(full, j) for j in range(8)]
        inblk = (lane >= r0) & (lane < r0 + 8)
        for i in range(b + 1, T // 8):
            acc = jnp.where(inblk, 0.0, rows[i])
            for j in range(8):
                acc = acc - later[i][j] * pieces[j]
            rows[i] = acc
        rs = lax.rsqrt(dvec)
        rs = rs * (1.5 - 0.5 * dvec * rs * rs)
        row = sub + r0
        scaled = low * rs
        inv_rows.append(jnp.where(lane < row, scaled, jnp.where(lane == row, rs, 0.0)))
        fac_rows.append(jnp.where(lane >= row, scaled, 0.0))
    return inv_rows, fac_rows


class Links:
    def __init__(self, a, pan, sbuf, abuf, bt, local, scat_s, scat_r, x_s, x_r, ag_s, ag_r, b_s, b_r, f_s, t_s, t_r, p_s, p_r, c_s, c_r):
        self.a, self.sbuf, self.abuf, self.bt, self.local = a, sbuf, abuf, bt, local
        self.pan, self.f_s, self.t_s, self.t_r = pan, f_s, t_s, t_r
        self.p_s, self.p_r, self.c_s, self.c_r = p_s, p_r, c_s, c_r
        self.scat_s, self.scat_r, self.x_s, self.x_r = scat_s, scat_r, x_s, x_r
        self.ag_s, self.ag_r, self.b_s, self.b_r = ag_s, ag_r, b_s, b_r
        self.pr, self.pc = lax.axis_index("pr"), lax.axis_index("pc")
        self.y, self.z, self.c = self.pc // 8, (self.pc // 2) % 4, self.pc % 2
        self.owner = self.pr == self.pc % 4
        self.src_pc = self.place(self.y, 2 * (self.z // 2) + self.pr // 2, self.pr % 2)
        self.from_self = self.src_pc == self.pc

    def copy(self, src, dst, send, recv, pr, pc):
        return pltpu.make_async_remote_copy(
            src_ref=src, dst_ref=dst, send_sem=send, recv_sem=recv, device_id={"pr": pr, "pc": pc}, device_id_type=MESH
        )

    def place(self, y, z, c):
        return (y * 4 + z) * 2 + c

    def barrier(self):
        sem = pltpu.get_barrier_semaphore()

        def signal(pr, pc):
            pl.semaphore_signal(sem, inc=1, device_id={"pr": pr, "pc": pc}, device_id_type=MESH)

        for n in range(1, 4):
            signal((self.pr + n) % 4, self.pc)
            signal(self.pr, self.place((self.y + n) % 4, self.z, self.c))
            signal(self.pr, self.place(self.y, (self.z + n) % 4, self.c))
        signal(self.pr, self.place(self.y, self.z, 1 - self.c))
        roots = [(self.pr == p) & (self.pc == q) for p, q in ROOTS]
        for p, q in ROOTS:

            @pl.when((self.pr == p) & (self.pc != q))
            def _():
                signal(p, q)

        @pl.when(jnp.logical_not(self.from_self))
        def _():
            signal(self.pr, self.src_pc)

        is_root = roots[0] | roots[1] | roots[2]

        for base, group in ((41, is_root), (10, jnp.logical_not(is_root))):
            for more, kind in ((3, self.owner), (0, jnp.logical_not(self.owner))):

                @pl.when(group & kind)
                def _():
                    pl.semaphore_wait(sem, base + more)

    def slab(self, x, d):
        return self.sbuf.at[x, d // 8, (d // 2) % 4, d % 2]

    def scatter_copy(self, x, d):
        src = self.a.at[pl.ds(pl.multiple_of(d * 64, 64), 64)]
        return self.copy(src, self.slab(x, d), self.scat_s.at[d], self.scat_r.at[x], ROOTS[x][0], d)

    def own_copy(self, x):
        d = ROOTS[x][1]
        return pltpu.make_async_copy(self.a.at[pl.ds(d * 64, 64)], self.slab(x, d), self.local.at[0])

    def each_other(self, x, act):
        p, q = ROOTS[x]

        @pl.when((self.pr == p) & (self.pc == q))
        def _():
            @pl.loop(0, 32)
            def _(d):
                @pl.when(d != q)
                def _():
                    act(self.scatter_copy(x, d))

    def scatter_start(self, x):
        p, q = ROOTS[x]
        self.each_other(x, lambda copy: copy.start())

        @pl.when((self.pr == p) & (self.pc == q))
        def _():
            self.own_copy(x).start()

    def x_copy(self, x, n):
        mine = self.slab(x, self.pc)
        return self.copy(mine, mine, self.x_s.at[x, n - 1], self.x_r.at[x], (self.pr + n) % 4, self.pc)

    def spread_start(self, x):
        p, q = ROOTS[x]

        @pl.when((self.pr == p) & (self.pc == q))
        def _():
            self.own_copy(x).wait()

        @pl.when((self.pr == p) & (self.pc != q))
        def _():
            self.scatter_copy(x, self.pc).wait_recv()

        @pl.when(self.pr == p)
        def _():
            for n in range(1, 4):
                self.x_copy(x, n).start()

    def spread_wait(self, x):
        @pl.when(self.pr != ROOTS[x][0])
        def _():
            self.x_copy(x, 1).wait_recv()

    def gather_copies(self, x, phase, arriving=False):
        y, z, c = self.y, self.z, self.c
        if phase == 2:
            oc = 1 - c
            ref = self.sbuf.at[x, :, :, oc if arriving else c]
            return [self.copy(ref, ref, self.ag_s.at[x, 12], self.ag_r.at[x, 12], self.pr, self.place(y, z, oc))]
        out = []
        for n in range(1, 4):
            m = (4 - n) % 4 if arriving else 0
            ym, zm = (y + m) % 4, (z + m) % 4
            if phase == 0:
                first = self.sbuf.at[x, ym, z, c, pl.ds(0, 32)]
                second = self.sbuf.at[x, y, zm, c, pl.ds(32, 32)]
                to_first, to_second = self.place((y + n) % 4, z, c), self.place(y, (z + n) % 4, c)
            else:
                first = self.sbuf.at[x, :, zm, c, pl.ds(0, 32)]
                second = self.sbuf.at[x, ym, :, c, pl.ds(32, 32)]
                to_first, to_second = self.place(y, (z + n) % 4, c), self.place((y + n) % 4, z, c)
            k = phase * 6 + (n - 1) * 2
            out.append(self.copy(first, first, self.ag_s.at[x, k], self.ag_r.at[x, k], self.pr, to_first))
            out.append(self.copy(second, second, self.ag_s.at[x, k + 1], self.ag_r.at[x, k + 1], self.pr, to_second))
        return out

    def gather_start(self, x, phase):
        for copy in self.gather_copies(x, phase):
            copy.start()

    def gather_wait(self, x, phase):
        for copy in self.gather_copies(x, phase, arriving=True):
            copy.wait_recv()

    def own_copy_in(self):
        return pltpu.make_async_copy(self.a.at[pl.ds(0, 4 * NB)], self.abuf, self.local.at[1])

    def own_start(self):
        @pl.when(self.pr < 2)
        def _():
            self.own_copy_in().start()

    def turn(self):
        for k in range(2):

            @pl.when(self.pr == k)
            def _():
                self.own_copy_in().wait()
                for s in range(4):
                    self.bt[k, s] = self.abuf[pl.ds(s, NB, stride=4), :].T

    def b_copy(self, k, s, way):
        ref, n = self.bt.at[k, s], 3 if way else 1
        return self.copy(ref, ref, self.b_s.at[s, way], self.b_r.at[k, s, 0], (self.pr + n) % 4, self.pc)

    def f_copy(self, k, s, way):
        ref, n = self.bt.at[k, s, pl.ds(64 * way, 64)], 3 if way else 1
        return self.copy(ref, ref, self.f_s.at[k, s], self.b_r.at[k, s, way], (self.pr + n) % 4, self.pc)

    def at_distance(self, k, n):
        return self.pr == (k + n) % 4

    def b_start(self, s):
        for k in range(2):

            @pl.when(self.at_distance(k, 0))
            def _():
                for way in range(2):
                    self.b_copy(k, s, way).start()

    def b_forward(self, s):
        for k in range(2):
            for way, n in ((0, 1), (1, 3)):

                @pl.when(self.at_distance(k, n))
                def _():
                    self.b_copy(k, s, way).wait_recv()
                    self.f_copy(k, s, way).start()

    def b_wait(self, s):
        for k in range(2):

            @pl.when(self.at_distance(k, 2))
            def _():
                for way in range(2):
                    self.f_copy(k, s, way).wait_recv()

    def b_finish(self, s):
        for k in range(2):

            @pl.when(self.at_distance(k, 0))
            def _():
                for way in range(2):
                    self.b_copy(k, s, way).wait_send()

            for way, n in ((0, 1), (1, 3)):

                @pl.when(self.at_distance(k, n))
                def _():
                    self.f_copy(k, s, way).wait_send()

    def t_half(self, k, s, core):
        z = self.z if k == 0 else 2 * (self.z // 2) + 1 - self.z % 2
        return self.bt.at[k, s, pl.ds(core * 64, 64)], self.pan.at[self.y, z, s, core], z

    def t_local(self, s):
        src, dst, _ = self.t_half(0, s, self.c)
        return pltpu.make_async_copy(src, dst, self.local.at[2 + s])

    def t_copies(self, s):
        out = []
        for i, (k, core) in enumerate(((0, 1 - self.c), (1, 0), (1, 1))):
            src, dst, z = self.t_half(k, s, core)
            out.append(self.copy(src, dst, self.t_s.at[s, i], self.t_r.at[s], self.pr, self.place(self.y, z, core)))
        return out

    def t_start(self, s):
        @pl.when(self.owner)
        def _():
            self.t_local(s).start()
            for copy in self.t_copies(s):
                copy.start()

    def t_wait(self, s):
        @pl.when(self.from_self)
        def _():
            self.t_local(s).wait()

        @pl.when(jnp.logical_not(self.from_self))
        def _():
            mine = self.pan.at[self.y, self.z, s, self.c]
            self.copy(mine, mine, self.t_s.at[s, 0], self.t_r.at[s], self.pr, self.src_pc).wait_recv()

    def ring_part(self, s, order, phase, v, half):
        first, rows = (0, 32) if half is None else (16 * half, 16)
        at = pl.ds(32 * order + first, rows)
        along_y = (order + phase) % 2 == 0
        if phase == 0:
            return self.pan.at[v, self.z, s, self.c, at] if along_y else self.pan.at[self.y, v, s, self.c, at]
        return self.pan.at[v, :, s, self.c, at] if along_y else self.pan.at[:, v, s, self.c, at]

    def ring_copies(self, s, phase, step, arriving=False):
        out = []
        for order in range(2):
            along_y = (order + phase) % 2 == 0
            me = self.y if along_y else self.z
            for way in range(2):
                n = 1 if way == 0 else 3
                to = (me + n) % 4
                dev = self.place(to, self.z, self.c) if along_y else self.place(self.y, to, self.c)
                back = (step + 1 if arriving else step) * (4 - n)
                ref = self.ring_part(s, order, phase, (me + back) % 4, None if step == 0 else way)
                k = ((order * 2 + phase) * 2 + step) * 2 + way
                out.append(self.copy(ref, ref, self.p_s.at[s, k], self.p_r.at[s, k], self.pr, dev))
        return out

    def core_copy(self, s, arriving=False):
        oc = 1 - self.c
        ref = self.pan.at[:, :, s, oc if arriving else self.c]
        return self.copy(ref, ref, self.c_s.at[s], self.c_r.at[s], self.pr, self.place(self.y, self.z, oc))

    def panel_stage(self, s, stage):
        if stage == 1:
            self.b_forward(s)
        elif stage == 2:
            self.b_wait(s)
            self.t_start(s)
        elif stage == 3:
            self.t_wait(s)
        elif stage < 8:
            for copy in self.ring_copies(s, (stage - 4) // 2, stage % 2, arriving=True):
                copy.wait_recv()
        else:
            self.core_copy(s, arriving=True).wait_recv()
        if 3 <= stage < 7:
            for copy in self.ring_copies(s, (stage - 3) // 2, (stage - 3) % 2):
                copy.start()
        elif stage == 7:
            self.core_copy(s).start()

    def panel_slot(self, slot):
        for s in range(4):
            if 1 <= slot - s <= 8:
                self.panel_stage(s, slot - s)

    def finish(self):
        for s in range(4):

            self.b_finish(s)

            @pl.when(self.owner)
            def _():
                for copy in self.t_copies(s):
                    copy.wait_send()

            for phase in range(2):
                for step in range(2):
                    for copy in self.ring_copies(s, phase, step):
                        copy.wait_send()
            self.core_copy(s).wait_send()
        for x in range(3):
            self.each_other(x, lambda copy: copy.wait_send())

            @pl.when(self.pr == ROOTS[x][0])
            def _():
                for n in range(1, 4):
                    self.x_copy(x, n).wait_send()

            for phase in range(3):
                for copy in self.gather_copies(x, phase):
                    copy.wait_send()


def spread_rows(ref):
    return [ref[pl.ds(c, NB, stride=4), :] for c in range(4)]


def factor_kernel(a_ref, top_ref, q_ref, pan, sbuf, abuf, bt, m, u, g, r, x, w, *sems):
    net = Links(a_ref, pan, sbuf, abuf, bt, *sems)
    pr, pc = net.pr, net.pc
    flat = sbuf.reshape(3, 4 * NB, T)
    net.own_start()
    net.barrier()
    net.scatter_start(0)
    net.turn()
    for s in range(2):
        net.b_start(s)
    net.spread_start(0)
    net.scatter_start(1)
    net.scatter_start(2)
    net.spread_wait(0)
    net.gather_start(0, 0)
    net.gather_wait(0, 0)
    net.gather_start(0, 1)
    net.spread_start(1)
    net.spread_start(2)
    net.gather_wait(0, 1)
    net.gather_start(0, 2)
    for i in (1, 2):
        net.spread_wait(i)
        net.gather_start(i, 0)
    net.panel_slot(1)
    net.b_start(2)
    net.gather_wait(0, 2)
    net.panel_slot(2)
    net.b_start(3)
    for c, piece in enumerate(spread_rows(flat.at[0])):
        m[0:NB, c * T : (c + 1) * T] = piece

    def after(t):
        if t == 0:
            for i in (1, 2):
                net.gather_wait(i, 0)
                net.gather_start(i, 1)
        elif t == 1:
            for i in (1, 2):
                net.gather_wait(i, 1)
                net.gather_start(i, 2)
        net.panel_slot(t + 3)

    def forward(lo, dst, rhs):
        for t in range(4):
            a, b = t * T, (t + 1) * T
            acc = rhs[a:b, :]
            if t:
                acc = acc - dot3(u[lo : lo + a, a:b], dst[0:a, :], 0, 0)
            dst[a:b, :] = dot3(g[lo + a : lo + b, :], acc)

    row = lax.broadcasted_iota(jnp.int32, (NB, NB), 0)
    col = lax.broadcasted_iota(jnp.int32, (NB, NB), 1)
    eye = jnp.where(row == col, 1.0, 0.0)

    def solve_second():
        for i in (1, 2):
            net.gather_wait(i, 2)
        for c, piece in enumerate(spread_rows(flat.at[1])):
            r[:, c * T : (c + 1) * T] = piece
            r[:, NB + c * T : NB + (c + 1) * T] = bt[0, c].T
        r[:, N2:] = eye
        forward(0, x, r)
        r[:, 0:N2] = dot3(x[:, 0:NB], x[:, 0:N2], 0, 0)
        for c, piece in enumerate(spread_rows(flat.at[2])):
            at, bat = slice(c * T, (c + 1) * T), slice(NB + c * T, NB + (c + 1) * T)
            m[NB:, at] = piece - r[:, at]
            r[:, at] = bt[1, c].T - r[:, bat]
        r[:, NB:N2] = eye

    @pl.loop(0, NT)
    def _(t):
        o = pl.multiple_of(t * T, T)
        oc = pl.multiple_of((t % 4) * T, T)
        rows = [m[pl.ds(o + 8 * i, 8), pl.ds(oc, T)] for i in range(T // 8)]
        inv_rows, fac_rows = factor_tile(rows)
        for i in range(T // 8):
            g[pl.ds(o + 8 * i, 8), :] = inv_rows[i]
            u[pl.ds(o + 8 * i, 8), pl.ds(oc, T)] = fac_rows[i]
        for ts in range(NT):

            @pl.when(t == ts)
            def _():
                if ts % 4 == 3:
                    if ts == 3:
                        solve_second()
                    else:
                        forward(NB, w, r.at[:, 0:N2])
                    after(ts)
                    return
                base = ts // 4 * NB
                a, b = ts % 4 * T, (ts % 4 + 1) * T
                piece = dot(g[base + a : base + b, :], m[base + a : base + b, b:])
                u[base + a : base + b, b:] = piece
                for i in range(ts % 4 + 1, 4):
                    lo = i * T - b
                    m[base + i * T : base + (i + 1) * T, i * T :] -= dot(piece[:, lo : lo + T], piece[:, lo:], 0, 0)
                after(ts)

    @pl.when(pr == 0)
    def _():
        top_ref[...] = x[:, NB:N2]

    @pl.when(pr > 0)
    def _():
        top_ref[...] = w[:, 0:NB]

    for k in range(2):

        @pl.when((pc == k) & (pr == k))
        def _():
            for i in range(NB // T):
                for j in range(NB // T):
                    if j <= i:
                        piece = u[k * NB + j * T : k * NB + (j + 1) * T, i * T : (i + 1) * T].T
                    else:
                        piece = jnp.zeros((T, T), jnp.float32)
                    top_ref[i * T : (i + 1) * T, j * T : (j + 1) * T] = piece

    @pl.when(pc < 2)
    def _():
        x[:, NB:N2] = jnp.where(pc == 0, -eye, 0.0)
        w[:, 0:NB] = jnp.where(pc == 1, -eye, 0.0)

    q_ref[NB:, :] = dot3(w[:, NB:N2], w[:, 0:NB], 0, 0)
    r[:, 0:NB] = x[:, NB:N2] - dot3(x[:, 0:NB], q_ref[NB:, :])
    q_ref[0:NB, :] = dot3(x[:, N2:], r[:, 0:NB], 0, 0)
    net.panel_slot(11)
    net.finish()


def factor(a):
    vmem = pl.BlockSpec(memory_space=pltpu.VMEM)
    f32 = jnp.float32
    dma = pltpu.SemaphoreType.DMA
    return pl.pallas_call(
        factor_kernel,
        out_shape=(
            jax.ShapeDtypeStruct((NB, NB), f32),
            jax.ShapeDtypeStruct((N2, NB), f32),
            jax.ShapeDtypeStruct((4, 4, 4, 2, 64, NB), f32),
        ),
        in_specs=[pl.BlockSpec(memory_space=pl.ANY)],
        out_specs=(vmem, vmem, pl.BlockSpec(memory_space=pl.ANY)),
        scratch_shapes=[
            pltpu.VMEM((3, 4, 4, 2, 64, T), f32),
            pltpu.VMEM((4 * NB, T), f32),
            pltpu.VMEM((2, 4, T, NB), f32),
            pltpu.VMEM((N2, NB), f32),
            pltpu.VMEM((N2, NB), f32),
            pltpu.VMEM((N2, T), f32),
            pltpu.VMEM((NB, N2 + NB), f32),
            pltpu.VMEM((NB, N2 + NB), f32),
            pltpu.VMEM((NB, N2), f32),
            dma((6,)),
            dma((32,)),
            dma((3,)),
            dma((3, 3)),
            dma((3,)),
            dma((3, 13)),
            dma((3, 13)),
            dma((4, 2)),
            dma((2, 4, 2)),
            dma((2, 4)),
            dma((4, 3)),
            dma((4,)),
            dma((4, 16)),
            dma((4, 16)),
            dma((4,)),
            dma((4,)),
        ],
        compiler_params=pltpu.CompilerParams(vmem_limit_bytes=48 << 20, collective_id=0, has_side_effects=True),
        cost_estimate=pl.CostEstimate(flops=60_000_000_000, bytes_accessed=10_000_000, transcendentals=0),
    )(a)


def split(x):
    hi = x.astype(jnp.bfloat16)
    return hi, (x - hi.astype(jnp.float32)).astype(jnp.bfloat16)


def mm(a, b):
    return lax.dot_general(a, b, (((1,), (0,)), ((), ())), preferred_element_type=jnp.float32)


def update_kernel(a_ref, p_ref, q_ref, top_ref, o_ref, qh, ql):
    l = pl.program_id(0)
    pr = lax.axis_index("pr")
    pc = lax.axis_index("pc")

    @pl.when(l == 0)
    def _():
        qh[...], ql[...] = split(q_ref[...])

    keep = jnp.where(pc < 2, 0.0, 1.0)
    acc = None
    for k in range(2):
        ph, plo = split(p_ref[0, k])
        at = pl.ds(pl.multiple_of((k + pr // 2) % 2 * NB, NB), NB)
        h, lo = qh[at, :], ql[at, :]
        part = mm(ph, h) + (mm(ph, lo) + mm(plo, h))
        acc = part if acc is None else acc + part
    for c in range(4):
        at = pl.ds(c, NB, stride=4)
        o_ref[at, :] = keep * a_ref[at, :] - acc[:, c * T : (c + 1) * T]

    @pl.when((l == 0) & ((pr == 0) | ((pr == 1) & (pc > 0))))
    def _():
        for c in range(4):
            o_ref[pl.ds(c, NB, stride=4), :] = top_ref[:, c * T : (c + 1) * T]


def update(a, p, q, top):
    return pl.pallas_call(
        update_kernel,
        grid=(8,),
        out_shape=jax.ShapeDtypeStruct(a.shape, jnp.float32),
        in_specs=[
            pl.BlockSpec((4 * NB, T), lambda l: (l, 0)),
            pl.BlockSpec((1, 2, NB, NB), lambda l: (l, 0, 0, 0)),
            pl.BlockSpec((N2, NB), lambda l: (0, 0)),
            pl.BlockSpec((NB, NB), lambda l: (0, 0)),
        ],
        out_specs=pl.BlockSpec((4 * NB, T), lambda l: (l, 0)),
        scratch_shapes=[pltpu.VMEM((N2, NB), jnp.bfloat16), pltpu.VMEM((N2, NB), jnp.bfloat16)],
        compiler_params=pltpu.CompilerParams(vmem_limit_bytes=48 << 20),
        cost_estimate=pl.CostEstimate(flops=13_000_000_000, bytes_accessed=34_000_000, transcendentals=0),
    )(a, p, q, top)


def body(matrix):
    flat = matrix.reshape(8 * NB * 4, T)
    top, q, panel = factor(flat)
    panel = panel.reshape(8, 2, NB, NB)
    return update(flat, panel, q, top).reshape(matrix.shape)


def solution(mesh):
    return jax.shard_map(
        body,
        mesh=mesh,
        in_specs=(P("pr", None, None, "pc", None, None),),
        out_specs=P("pr", None, None, "pc", None, None),
        check_vma=False,
    )
```

```python
import jax
import jax.numpy as jnp
from jax import lax
from jax.experimental import pallas as pl
from jax.experimental.pallas import tpu as pltpu
from jax.sharding import PartitionSpec as P
HI = lax.Precision.HIGHEST
T = 128
NT = 8
NB = 512
HB = 256
N2 = 1024
MESH = pl.DeviceIdType.MESH
ROOTS = ((0, 0), (0, 1), (1, 1))


def dot(a, b, ca=1, cb=0):
    return lax.dot_general(a, b, (((ca,), (cb,)), ((), ())), precision=HI, preferred_element_type=jnp.float32)


def dot3(a, b, ca=1, cb=0):
    (ah, al), (bh, bl) = split(a), split(b)

    def one(p, q):
        return lax.dot_general(p, q, (((ca,), (cb,)), ((), ())), preferred_element_type=jnp.float32)

    return one(ah, bh) + (one(ah, bl) + one(al, bh))


def sub_bcast(x, j):
    return jnp.broadcast_to(x[j : j + 1, :], (8, T))


def lane_bcast(x, j):
    return jnp.broadcast_to(x[:, j : j + 1], (8, T))


def factor_tile(rows):
    sub = lax.broadcasted_iota(jnp.int32, (8, T), 0)
    lane = lax.broadcasted_iota(jnp.int32, (8, T), 1)
    inv_rows, fac_rows = [], []
    for b in range(T // 8):
        r0 = 8 * b
        low = rows[b]
        full = rows[b]
        cols = [lane_bcast(rows[b], r0 + j) for j in range(8)]
        later = {i: [lane_bcast(rows[i], r0 + j) for j in range(8)] for i in range(b + 1, T // 8)}
        dvec = jnp.zeros((8, T), jnp.float32)
        rvec = jnp.zeros((8, T), jnp.float32)
        for j in range(8):
            d = sub_bcast(cols[j], j)
            rinv = 1.0 / d
            f = cols[j] * rinv
            here = lane == r0 + j
            fg = jnp.where(sub == j, 0.0, f)
            fl = jnp.where(sub > j, f, 0.0)
            for jj in range(j + 1, 8):
                cols[jj] = cols[jj] - fg * sub_bcast(cols[jj], j)
            low_now = jnp.where(here & (sub > j), 0.0, low)
            lrow = jnp.where(here, 1.0, sub_bcast(low, j))
            low = low_now - fl * lrow
            grow = jnp.where(here, 1.0, sub_bcast(full, j))
            full = jnp.where(here, jnp.where(sub == j, 1.0, 0.0), full) - fg * grow
            dvec = jnp.where(sub == j, d, dvec)
            rvec = jnp.where(sub == j, rinv, rvec)
        full = full * rvec
        pieces = [sub_bcast(full, j) for j in range(8)]
        inblk = (lane >= r0) & (lane < r0 + 8)
        for i in range(b + 1, T // 8):
            acc = jnp.where(inblk, 0.0, rows[i])
            for j in range(8):
                acc = acc - later[i][j] * pieces[j]
            rows[i] = acc
        rs = lax.rsqrt(dvec)
        rs = rs * (1.5 - 0.5 * dvec * rs * rs)
        row = sub + r0
        scaled = low * rs
        inv_rows.append(jnp.where(lane < row, scaled, jnp.where(lane == row, rs, 0.0)))
        fac_rows.append(jnp.where(lane >= row, scaled, 0.0))
    return inv_rows, fac_rows


class Links:
    def __init__(self, a, pan, sbuf, abuf, bt, local, scat_s, scat_r, x_s, x_r, ag_s, ag_r, b_s, b_r, f_s, t_s, t_r, p_s, p_r, c_s, c_r):
        self.a, self.sbuf, self.abuf, self.bt, self.local = a, sbuf, abuf, bt, local
        self.pan, self.f_s, self.t_s, self.t_r = pan, f_s, t_s, t_r
        self.p_s, self.p_r, self.c_s, self.c_r = p_s, p_r, c_s, c_r
        self.scat_s, self.scat_r, self.x_s, self.x_r = scat_s, scat_r, x_s, x_r
        self.ag_s, self.ag_r, self.b_s, self.b_r = ag_s, ag_r, b_s, b_r
        self.pr, self.pc = lax.axis_index("pr"), lax.axis_index("pc")
        self.y, self.z, self.c = self.pc // 8, (self.pc // 2) % 4, self.pc % 2
        self.owner = self.pr == self.pc % 4
        self.src_pc = self.place(self.y, 2 * (self.z // 2) + self.pr // 2, self.pr % 2)
        self.from_self = self.src_pc == self.pc

    def copy(self, src, dst, send, recv, pr, pc):
        return pltpu.make_async_remote_copy(
            src_ref=src, dst_ref=dst, send_sem=send, recv_sem=recv, device_id={"pr": pr, "pc": pc}, device_id_type=MESH
        )

    def place(self, y, z, c):
        return (y * 4 + z) * 2 + c

    def barrier(self):
        sem = pltpu.get_barrier_semaphore()

        def signal(pr, pc):
            pl.semaphore_signal(sem, inc=1, device_id={"pr": pr, "pc": pc}, device_id_type=MESH)

        for n in range(1, 4):
            signal((self.pr + n) % 4, self.pc)
            signal(self.pr, self.place((self.y + n) % 4, self.z, self.c))
            signal(self.pr, self.place(self.y, (self.z + n) % 4, self.c))
        signal(self.pr, self.place(self.y, self.z, 1 - self.c))
        roots = [(self.pr == p) & (self.pc == q) for p, q in ROOTS]
        for p, q in ROOTS:

            @pl.when((self.pr == p) & (self.pc != q))
            def _():
                signal(p, q)

        @pl.when(jnp.logical_not(self.from_self))
        def _():
            signal(self.pr, self.src_pc)

        is_root = roots[0] | roots[1] | roots[2]

        for base, group in ((41, is_root), (10, jnp.logical_not(is_root))):
            for more, kind in ((3, self.owner), (0, jnp.logical_not(self.owner))):

                @pl.when(group & kind)
                def _():
                    pl.semaphore_wait(sem, base + more)

    def slab(self, x, d):
        return self.sbuf.at[x, d // 8, (d // 2) % 4, d % 2]

    def scatter_copy(self, x, d):
        src = self.a.at[pl.ds(pl.multiple_of(d * 64, 64), 64)]
        return self.copy(src, self.slab(x, d), self.scat_s.at[d], self.scat_r.at[x], ROOTS[x][0], d)

    def own_copy(self, x):
        d = ROOTS[x][1]
        return pltpu.make_async_copy(self.a.at[pl.ds(d * 64, 64)], self.slab(x, d), self.local.at[0])

    def each_other(self, x, act):
        p, q = ROOTS[x]

        @pl.when((self.pr == p) & (self.pc == q))
        def _():
            @pl.loop(0, 32)
            def _(d):
                @pl.when(d != q)
                def _():
                    act(self.scatter_copy(x, d))

    def scatter_start(self, x):
        p, q = ROOTS[x]
        self.each_other(x, lambda copy: copy.start())

        @pl.when((self.pr == p) & (self.pc == q))
        def _():
            self.own_copy(x).start()

    def x_copy(self, x, n):
        mine = self.slab(x, self.pc)
        return self.copy(mine, mine, self.x_s.at[x, n - 1], self.x_r.at[x], (self.pr + n) % 4, self.pc)

    def spread_start(self, x):
        p, q = ROOTS[x]

        @pl.when((self.pr == p) & (self.pc == q))
        def _():
            self.own_copy(x).wait()

        @pl.when((self.pr == p) & (self.pc != q))
        def _():
            self.scatter_copy(x, self.pc).wait_recv()

        @pl.when(self.pr == p)
        def _():
            for n in range(1, 4):
                self.x_copy(x, n).start()

    def spread_wait(self, x):
        @pl.when(self.pr != ROOTS[x][0])
        def _():
            self.x_copy(x, 1).wait_recv()

    def gather_copies(self, x, phase, arriving=False):
        y, z, c = self.y, self.z, self.c
        if phase == 2:
            oc = 1 - c
            ref = self.sbuf.at[x, :, :, oc if arriving else c]
            return [self.copy(ref, ref, self.ag_s.at[x, 12], self.ag_r.at[x, 12], self.pr, self.place(y, z, oc))]
        out = []
        for n in range(1, 4):
            m = (4 - n) % 4 if arriving else 0
            ym, zm = (y + m) % 4, (z + m) % 4
            if phase == 0:
                first = self.sbuf.at[x, ym, z, c, pl.ds(0, 32)]
                second = self.sbuf.at[x, y, zm, c, pl.ds(32, 32)]
                to_first, to_second = self.place((y + n) % 4, z, c), self.place(y, (z + n) % 4, c)
            else:
                first = self.sbuf.at[x, :, zm, c, pl.ds(0, 32)]
                second = self.sbuf.at[x, ym, :, c, pl.ds(32, 32)]
                to_first, to_second = self.place(y, (z + n) % 4, c), self.place((y + n) % 4, z, c)
            k = phase * 6 + (n - 1) * 2
            out.append(self.copy(first, first, self.ag_s.at[x, k], self.ag_r.at[x, k], self.pr, to_first))
            out.append(self.copy(second, second, self.ag_s.at[x, k + 1], self.ag_r.at[x, k + 1], self.pr, to_second))
        return out

    def gather_start(self, x, phase):
        for copy in self.gather_copies(x, phase):
            copy.start()

    def gather_wait(self, x, phase):
        for copy in self.gather_copies(x, phase, arriving=True):
            copy.wait_recv()

    def own_copy_in(self):
        return pltpu.make_async_copy(self.a.at[pl.ds(0, 4 * NB)], self.abuf, self.local.at[1])

    def own_start(self):
        @pl.when(self.pr < 2)
        def _():
            self.own_copy_in().start()

    def turn(self):
        for k in range(2):

            @pl.when(self.pr == k)
            def _():
                self.own_copy_in().wait()
                for s in range(4):
                    self.bt[k, s] = self.abuf[pl.ds(s, NB, stride=4), :].T

    def b_copy(self, k, s, way):
        ref, n = self.bt.at[k, s], 3 if way else 1
        return self.copy(ref, ref, self.b_s.at[s, way], self.b_r.at[k, s, 0], (self.pr + n) % 4, self.pc)

    def f_copy(self, k, s, way):
        ref, n = self.bt.at[k, s, pl.ds(64 * way, 64)], 3 if way else 1
        return self.copy(ref, ref, self.f_s.at[k, s], self.b_r.at[k, s, way], (self.pr + n) % 4, self.pc)

    def at_distance(self, k, n):
        return self.pr == (k + n) % 4

    def b_start(self, s):
        for k in range(2):

            @pl.when(self.at_distance(k, 0))
            def _():
                for way in range(2):
                    self.b_copy(k, s, way).start()

    def b_forward(self, s):
        for k in range(2):
            for way, n in ((0, 1), (1, 3)):

                @pl.when(self.at_distance(k, n))
                def _():
                    self.b_copy(k, s, way).wait_recv()
                    self.f_copy(k, s, way).start()

    def b_wait(self, s):
        for k in range(2):

            @pl.when(self.at_distance(k, 2))
            def _():
                for way in range(2):
                    self.f_copy(k, s, way).wait_recv()

    def b_finish(self, s):
        for k in range(2):

            @pl.when(self.at_distance(k, 0))
            def _():
                for way in range(2):
                    self.b_copy(k, s, way).wait_send()

            for way, n in ((0, 1), (1, 3)):

                @pl.when(self.at_distance(k, n))
                def _():
                    self.f_copy(k, s, way).wait_send()

    def t_half(self, k, s, core):
        z = self.z if k == 0 else 2 * (self.z // 2) + 1 - self.z % 2
        return self.bt.at[k, s, pl.ds(core * 64, 64)], self.pan.at[self.y, z, s, core], z

    def t_local(self, s):
        src, dst, _ = self.t_half(0, s, self.c)
        return pltpu.make_async_copy(src, dst, self.local.at[2 + s])

    def t_copies(self, s):
        out = []
        for i, (k, core) in enumerate(((0, 1 - self.c), (1, 0), (1, 1))):
            src, dst, z = self.t_half(k, s, core)
            out.append(self.copy(src, dst, self.t_s.at[s, i], self.t_r.at[s], self.pr, self.place(self.y, z, core)))
        return out

    def t_start(self, s):
        @pl.when(self.owner)
        def _():
            self.t_local(s).start()
            for copy in self.t_copies(s):
                copy.start()

    def t_wait(self, s):
        @pl.when(self.from_self)
        def _():
            self.t_local(s).wait()

        @pl.when(jnp.logical_not(self.from_self))
        def _():
            mine = self.pan.at[self.y, self.z, s, self.c]
            self.copy(mine, mine, self.t_s.at[s, 0], self.t_r.at[s], self.pr, self.src_pc).wait_recv()

    def ring_part(self, s, order, phase, v, half):
        first, rows = (0, 32) if half is None else (16 * half, 16)
        at = pl.ds(32 * order + first, rows)
        along_y = (order + phase) % 2 == 0
        if phase == 0:
            return self.pan.at[v, self.z, s, self.c, at] if along_y else self.pan.at[self.y, v, s, self.c, at]
        return self.pan.at[v, :, s, self.c, at] if along_y else self.pan.at[:, v, s, self.c, at]

    def ring_copies(self, s, phase, step, arriving=False):
        out = []
        for order in range(2):
            along_y = (order + phase) % 2 == 0
            me = self.y if along_y else self.z
            for way in range(2):
                n = 1 if way == 0 else 3
                to = (me + n) % 4
                dev = self.place(to, self.z, self.c) if along_y else self.place(self.y, to, self.c)
                back = (step + 1 if arriving else step) * (4 - n)
                ref = self.ring_part(s, order, phase, (me + back) % 4, None if step == 0 else way)
                k = ((order * 2 + phase) * 2 + step) * 2 + way
                out.append(self.copy(ref, ref, self.p_s.at[s, k], self.p_r.at[s, k], self.pr, dev))
        return out

    def core_copy(self, s, arriving=False):
        oc = 1 - self.c
        ref = self.pan.at[:, :, s, oc if arriving else self.c]
        return self.copy(ref, ref, self.c_s.at[s], self.c_r.at[s], self.pr, self.place(self.y, self.z, oc))

    def panel_stage(self, s, stage):
        if stage == 1:
            self.b_forward(s)
        elif stage == 2:
            self.b_wait(s)
            self.t_start(s)
        elif stage == 3:
            self.t_wait(s)
        elif stage < 8:
            for copy in self.ring_copies(s, (stage - 4) // 2, stage % 2, arriving=True):
                copy.wait_recv()
        else:
            self.core_copy(s, arriving=True).wait_recv()
        if 3 <= stage < 7:
            for copy in self.ring_copies(s, (stage - 3) // 2, (stage - 3) % 2):
                copy.start()
        elif stage == 7:
            self.core_copy(s).start()

    def panel_slot(self, slot):
        for s in range(4):
            if 1 <= slot - s <= 8:
                self.panel_stage(s, slot - s)

    def finish(self):
        for s in range(4):

            self.b_finish(s)

            @pl.when(self.owner)
            def _():
                for copy in self.t_copies(s):
                    copy.wait_send()

            for phase in range(2):
                for step in range(2):
                    for copy in self.ring_copies(s, phase, step):
                        copy.wait_send()
            self.core_copy(s).wait_send()
        for x in range(3):
            self.each_other(x, lambda copy: copy.wait_send())

            @pl.when(self.pr == ROOTS[x][0])
            def _():
                for n in range(1, 4):
                    self.x_copy(x, n).wait_send()

            for phase in range(3):
                for copy in self.gather_copies(x, phase):
                    copy.wait_send()


def spread_rows(ref):
    return [ref[pl.ds(c, NB, stride=4), :] for c in range(4)]


def factor_kernel(a_ref, top_ref, q_ref, pan, sbuf, abuf, bt, m, u, g, r, x, w, *sems):
    net = Links(a_ref, pan, sbuf, abuf, bt, *sems)
    pr, pc = net.pr, net.pc
    flat = sbuf.reshape(3, 4 * NB, T)
    net.own_start()
    net.barrier()
    net.scatter_start(0)
    net.turn()
    for s in range(2):
        net.b_start(s)
    net.spread_start(0)
    net.scatter_start(1)
    net.scatter_start(2)
    net.spread_wait(0)
    net.gather_start(0, 0)
    net.gather_wait(0, 0)
    net.gather_start(0, 1)
    net.spread_start(1)
    net.spread_start(2)
    net.gather_wait(0, 1)
    net.gather_start(0, 2)
    for i in (1, 2):
        net.spread_wait(i)
        net.gather_start(i, 0)
    net.panel_slot(1)
    net.b_start(2)
    net.gather_wait(0, 2)
    net.panel_slot(2)
    net.b_start(3)
    for c, piece in enumerate(spread_rows(flat.at[0])):
        m[0:NB, c * T : (c + 1) * T] = piece

    def after(t):
        if t == 0:
            for i in (1, 2):
                net.gather_wait(i, 0)
                net.gather_start(i, 1)
        elif t == 1:
            for i in (1, 2):
                net.gather_wait(i, 1)
                net.gather_start(i, 2)
        net.panel_slot(t + 3)

    def forward(lo, dst, rhs):
        for t in range(4):
            a, b = t * T, (t + 1) * T
            acc = rhs[a:b, :]
            if t:
                acc = acc - dot3(u[lo : lo + a, a:b], dst[0:a, :], 0, 0)
            dst[a:b, :] = dot3(g[lo + a : lo + b, :], acc)

    row = lax.broadcasted_iota(jnp.int32, (NB, NB), 0)
    col = lax.broadcasted_iota(jnp.int32, (NB, NB), 1)
    eye = jnp.where(row == col, 1.0, 0.0)

    def solve_second():
        for i in (1, 2):
            net.gather_wait(i, 2)
        for c, piece in enumerate(spread_rows(flat.at[1])):
            r[:, c * T : (c + 1) * T] = piece
            r[:, NB + c * T : NB + (c + 1) * T] = bt[0, c].T
        r[:, N2:] = eye
        forward(0, x, r)
        r[:, 0:N2] = dot3(x[:, 0:NB], x[:, 0:N2], 0, 0)
        for c, piece in enumerate(spread_rows(flat.at[2])):
            at, bat = slice(c * T, (c + 1) * T), slice(NB + c * T, NB + (c + 1) * T)
            m[NB:, at] = piece - r[:, at]
            r[:, at] = bt[1, c].T - r[:, bat]
        r[:, NB:N2] = eye

    @pl.loop(0, NT)
    def _(t):
        o = pl.multiple_of(t * T, T)
        oc = pl.multiple_of((t % 4) * T, T)
        rows = [m[pl.ds(o + 8 * i, 8), pl.ds(oc, T)] for i in range(T // 8)]
        inv_rows, fac_rows = factor_tile(rows)
        for i in range(T // 8):
            g[pl.ds(o + 8 * i, 8), :] = inv_rows[i]
            u[pl.ds(o + 8 * i, 8), pl.ds(oc, T)] = fac_rows[i]
        for ts in range(NT):

            @pl.when(t == ts)
            def _():
                if ts % 4 == 3:
                    if ts == 3:
                        solve_second()
                    else:
                        forward(NB, w, r.at[:, 0:N2])
                    after(ts)
                    return
                base = ts // 4 * NB
                a, b = ts % 4 * T, (ts % 4 + 1) * T
                piece = dot(g[base + a : base + b, :], m[base + a : base + b, b:])
                u[base + a : base + b, b:] = piece
                for i in range(ts % 4 + 1, 4):
                    lo = i * T - b
                    m[base + i * T : base + (i + 1) * T, i * T :] -= dot(piece[:, lo : lo + T], piece[:, lo:], 0, 0)
                after(ts)

    @pl.when(pr == 0)
    def _():
        top_ref[...] = x[:, NB:N2]

    @pl.when(pr > 0)
    def _():
        top_ref[...] = w[:, 0:NB]

    for k in range(2):

        @pl.when((pc == k) & (pr == k))
        def _():
            for i in range(NB // T):
                for j in range(NB // T):
                    if j <= i:
                        piece = u[k * NB + j * T : k * NB + (j + 1) * T, i * T : (i + 1) * T].T
                    else:
                        piece = jnp.zeros((T, T), jnp.float32)
                    top_ref[i * T : (i + 1) * T, j * T : (j + 1) * T] = piece

    @pl.when(pc < 2)
    def _():
        x[:, NB:N2] = jnp.where(pc == 0, -eye, 0.0)
        w[:, 0:NB] = jnp.where(pc == 1, -eye, 0.0)

    q_ref[NB:, :] = dot3(w[:, NB:N2], w[:, 0:NB], 0, 0)
    r[:, 0:NB] = x[:, NB:N2] - dot3(x[:, 0:NB], q_ref[NB:, :])
    q_ref[0:NB, :] = dot3(x[:, N2:], r[:, 0:NB], 0, 0)
    net.panel_slot(11)
    net.finish()


def factor(a):
    vmem = pl.BlockSpec(memory_space=pltpu.VMEM)
    f32 = jnp.float32
    dma = pltpu.SemaphoreType.DMA
    return pl.pallas_call(
        factor_kernel,
        out_shape=(
            jax.ShapeDtypeStruct((NB, NB), f32),
            jax.ShapeDtypeStruct((N2, NB), f32),
            jax.ShapeDtypeStruct((4, 4, 4, 2, 64, NB), f32),
        ),
        in_specs=[pl.BlockSpec(memory_space=pl.ANY)],
        out_specs=(vmem, vmem, pl.BlockSpec(memory_space=pl.ANY)),
        scratch_shapes=[
            pltpu.VMEM((3, 4, 4, 2, 64, T), f32),
            pltpu.VMEM((4 * NB, T), f32),
            pltpu.VMEM((2, 4, T, NB), f32),
            pltpu.VMEM((N2, NB), f32),
            pltpu.VMEM((N2, NB), f32),
            pltpu.VMEM((N2, T), f32),
            pltpu.VMEM((NB, N2 + NB), f32),
            pltpu.VMEM((NB, N2 + NB), f32),
            pltpu.VMEM((NB, N2), f32),
            dma((6,)),
            dma((32,)),
            dma((3,)),
            dma((3, 3)),
            dma((3,)),
            dma((3, 13)),
            dma((3, 13)),
            dma((4, 2)),
            dma((2, 4, 2)),
            dma((2, 4)),
            dma((4, 3)),
            dma((4,)),
            dma((4, 16)),
            dma((4, 16)),
            dma((4,)),
            dma((4,)),
        ],
        compiler_params=pltpu.CompilerParams(vmem_limit_bytes=48 << 20, collective_id=0, has_side_effects=True),
        cost_estimate=pl.CostEstimate(flops=60_000_000_000, bytes_accessed=10_000_000, transcendentals=0),
    )(a)


def split(x):
    hi = x.astype(jnp.bfloat16)
    return hi, (x - hi.astype(jnp.float32)).astype(jnp.bfloat16)


def mm(a, b):
    return lax.dot_general(a, b, (((1,), (0,)), ((), ())), preferred_element_type=jnp.float32)


def update_kernel(a_ref, p_ref, q_ref, top_ref, o_ref, qh, ql):
    l = pl.program_id(0)
    pr = lax.axis_index("pr")
    pc = lax.axis_index("pc")

    @pl.when(l == 0)
    def _():
        qh[...], ql[...] = split(q_ref[...])

    keep = jnp.where(pc < 2, 0.0, 1.0)
    acc = None
    for k in range(2):
        ph, plo = split(p_ref[0, k])
        at = pl.ds(pl.multiple_of((k + pr // 2) % 2 * NB, NB), NB)
        h, lo = qh[at, :], ql[at, :]
        part = mm(ph, h) + (mm(ph, lo) + mm(plo, h))
        acc = part if acc is None else acc + part
    for c in range(4):
        at = pl.ds(c, HB, stride=4)
        o_ref[at, :] = keep * a_ref[at, :] - acc[:, c * T : (c + 1) * T]

    @pl.when((l < 2) & ((pr == 0) | ((pr == 1) & (pc > 0))))
    def _():
        for c in range(4):
            o_ref[pl.ds(c, HB, stride=4), :] = top_ref[:, c * T : (c + 1) * T]


def update(a, p, q, top):
    return pl.pallas_call(
        update_kernel,
        grid=(16,),
        out_shape=jax.ShapeDtypeStruct(a.shape, jnp.float32),
        in_specs=[
            pl.BlockSpec((4 * HB, T), lambda l: (l, 0)),
            pl.BlockSpec((1, 2, HB, NB), lambda l: (l // 2, 0, l % 2, 0)),
            pl.BlockSpec((N2, NB), lambda l: (0, 0)),
            pl.BlockSpec((HB, NB), lambda l: (jnp.minimum(l, 1), 0)),
        ],
        out_specs=pl.BlockSpec((4 * HB, T), lambda l: (l, 0)),
        scratch_shapes=[pltpu.VMEM((N2, NB), jnp.bfloat16), pltpu.VMEM((N2, NB), jnp.bfloat16)],
        compiler_params=pltpu.CompilerParams(vmem_limit_bytes=48 << 20),
        cost_estimate=pl.CostEstimate(flops=13_000_000_000, bytes_accessed=34_000_000, transcendentals=0),
    )(a, p, q, top)


def body(matrix):
    flat = matrix.reshape(8 * NB * 4, T)
    top, q, panel = factor(flat)
    panel = panel.reshape(8, 2, NB, NB)
    return update(flat, panel, q, top).reshape(matrix.shape)


def solution(mesh):
    return jax.shard_map(
        body,
        mesh=mesh,
        in_specs=(P("pr", None, None, "pc", None, None),),
        out_specs=P("pr", None, None, "pc", None, None),
        check_vma=False,
    )
```
